32 devices in a mesh: dp: 8 (over y, x, core), tensor: 4 (over z).
Axes of the slice: x: 2, y: 2, z: 4, core: 2. Of those that a mesh axis runs over, the one named last changes fastest.
Arguments:
- tokens: bfloat16 [4096, 2048], P(('dp', 'tensor')), may hold values from -6 to 6
- seq_lengths: int32 [24], replicated, may hold values from 64 to 384, as said below
- seq_group: int32 [24], replicated, may hold values from 0 to 7, as said below
- attn_gain: bfloat16 [2048], P('dp'), may hold values from 0.099609375 to 1.8984375
- w_query: bfloat16 [2048, 2048], P('dp', 'tensor'), may hold values from -0.125 to 0.125
- w_key: bfloat16 [2048, 512], P('dp', 'tensor'), may hold values from -0.125 to 0.125
- w_value: bfloat16 [2048, 512], P('dp', 'tensor'), may hold values from -0.125 to 0.125
- w_out: bfloat16 [2048, 2048], P('tensor', 'dp'), may hold values from -1 to 1
- mlp_gain: bfloat16 [2048], P('dp'), may hold values from 0.099609375 to 1.8984375
- w_gate: bfloat16 [2048, 8192], P('dp', 'tensor'), may hold values from -0.125 to 0.125
- w_up: bfloat16 [2048, 8192], P('dp', 'tensor'), may hold values from -0.125 to 0.125
- w_down: bfloat16 [8192, 2048], P('tensor', 'dp'), may hold values from -0.125 to 0.125
- cotangent: bfloat16 [4096, 2048], P(('dp', 'tensor')), may hold values from -6 to 6
Outputs:
- block_out: bfloat16 [4096, 2048], P(('dp', 'tensor'))
- grad_tokens: bfloat16 [4096, 2048], P(('dp', 'tensor'))
- grad_attn_gain: float32 [2048], P('dp')
- grad_w_query: float32 [2048, 2048], P('dp', 'tensor')
- grad_w_key: float32 [2048, 512], P('dp', 'tensor')
- grad_w_value: float32 [2048, 512], P('dp', 'tensor')
- grad_w_out: float32 [2048, 2048], P('tensor', 'dp')
- grad_mlp_gain: float32 [2048], P('dp')
- grad_w_gate: float32 [2048, 8192], P('dp', 'tensor')
- grad_w_up: float32 [2048, 8192], P('dp', 'tensor')
- grad_w_down: float32 [8192, 2048], P('tensor', 'dp')
The draws below stay inside these ranges and needn't reach their ends.
Inputs may be any that keep to these rules, and one draw needn't show every extreme that they name: `seq_group`: each data group gets exactly 3 sequences. `seq_lengths`: the sequences of one data group fill at most its 512 rows, in at least one group exactly; in every group one sequence starts within the group's first 128 rows and ends within its last 128 rows.
All inputs are finite; a program needn't handle non-finite values.
Results may differ from the reference program's by a relative error of at most 0.02.
Values may be sent and summed in bfloat16 or wider, within the bound.
No kernel may reach another device: no remote copies, remote signals or barrier semaphores. Data moves between devices by JAX's collectives and lax.ppermute only.
A program may use at most 128 MiB of HBM per device.

```python
import math
import jax
import jax.numpy as jnp
from jax import lax

D = 2048
HEADS = 32
KV_HEADS = 8
HEAD_DIM = 64
FF = 8192
TOK_DEV = 128
SLOTS = 3
MIN_LEN = 64
GROUP_TOK = 512
TOKENS = 4096
N_DP = 8


def pack_plan(key):
    slot_key, pad_key, first_key, last_key, full_key = jax.random.split(key, 5)
    order = jax.random.permutation(slot_key, SLOTS * N_DP)
    group_of = (order % N_DP).astype(jnp.int32)
    fullest = jax.random.randint(full_key, (), 0, N_DP)
    is_full = jnp.arange(N_DP) == fullest
    top_pad = (TOK_DEV - MIN_LEN) // 4
    padding = jnp.where(is_full, 0, jax.random.randint(pad_key, (N_DP,), 0, top_pad + 1))
    first_len = jnp.where(is_full, MIN_LEN, jax.random.randint(first_key, (N_DP,), MIN_LEN, TOK_DEV))
    last_room = TOK_DEV - MIN_LEN - padding
    last_draw = jax.random.randint(last_key, (N_DP,), 0, TOK_DEV)
    last_len = jnp.where(is_full, MIN_LEN, MIN_LEN + last_draw % last_room)
    long_len = GROUP_TOK - padding - first_len - last_len
    table = jnp.stack([first_len, long_len, last_len], axis=1)
    seq_ids = jnp.arange(SLOTS * N_DP)
    same = (group_of[None, :] == group_of[:, None]) & (seq_ids[None, :] < seq_ids[:, None])
    rank_of = jnp.sum(same.astype(jnp.int32), axis=1)
    lengths = table[group_of, rank_of]
    return (group_of, lengths.astype(jnp.int32))


def draw_seq_lengths(key, part):
    return pack_plan(key)[1]


def draw_seq_group(key, part):
    return pack_plan(key)[0]


def level_of(stream_key, shape, shards, least, largest):
    def one(dim, shards_of):
        steps = jax.random.uniform(jax.random.fold_in(jax.random.fold_in(stream_key, 6), dim), (shards_of,), jnp.float32, least / len(shards), largest / len(shards))
        return jnp.repeat(jnp.exp(steps), shape[dim] // shards_of).reshape((-1,) + (1,) * (len(shape) - dim - 1))

    level = one(*shards[0])
    for cut in shards[1:]:
        level = level * one(*cut)
    return level


def bell_draw(rng, shape, deviation, limit, pieces=(), kind=jnp.bfloat16):
    array = deviation * jax.random.normal(rng, shape, jnp.float32)
    if pieces:
        array = array * level_of(rng, shape, pieces, -0.22, 0.18)
    return jnp.clip(array, -limit, limit).astype(kind)


def setup_inputs(seed: int = 0) -> dict:
    arg_keys = jax.random.split(jax.random.key(seed), 14)
    return {
        "tokens": bell_draw(arg_keys[0], (TOKENS, D), 1.0, 6.0, ((0, 32),)),
        "seq_lengths": draw_seq_lengths(jax.random.fold_in(arg_keys[13], 71), 0),
        "seq_group": draw_seq_group(jax.random.fold_in(arg_keys[13], 71), 0),
        "attn_gain": jnp.clip(1.0 + 0.18 * jax.random.normal(arg_keys[3], (D,), jnp.float32), 0.099609375, 1.8984375).astype(jnp.bfloat16),
        "w_query": bell_draw(arg_keys[4], (D, HEADS * HEAD_DIM), D ** -0.5, 0.125, ((0, 8), (1, 4))),
        "w_key": bell_draw(arg_keys[5], (D, KV_HEADS * HEAD_DIM), D ** -0.5, 0.125, ((0, 8), (1, 4))),
        "w_value": bell_draw(arg_keys[6], (D, KV_HEADS * HEAD_DIM), D ** -0.5, 0.125, ((0, 8), (1, 4))),
        "w_out": bell_draw(arg_keys[7], (HEADS * HEAD_DIM, D), 32 ** -0.5, 1.0, ((0, 4), (1, 8))),
        "mlp_gain": jnp.clip(1.0 + 0.18 * jax.random.normal(arg_keys[8], (D,), jnp.float32), 0.099609375, 1.8984375).astype(jnp.bfloat16),
        "w_gate": bell_draw(arg_keys[9], (D, FF), D ** -0.5, 0.125, ((0, 8), (1, 4))),
        "w_up": bell_draw(arg_keys[10], (D, FF), D ** -0.5, 0.125, ((0, 8), (1, 4))),
        "w_down": bell_draw(arg_keys[11], (FF, D), (FF // 4) ** -0.5, 0.125, ((0, 4), (1, 8))),
        "cotangent": bell_draw(arg_keys[12], (TOKENS, D), 1.0, 6.0, ((0, 32),)),
    }


@jax.custom_vjp
def low(v):
    return lax.optimization_barrier(v.astype(jnp.bfloat16)).astype(jnp.float32)

@jax.custom_vjp
def low_back(v):
    return v

def low_keep(v):
    return (low(v), None)

def low_pass(kept, grad):
    return (grad,)

def back_keep(v):
    return (v, None)

def back_low(kept, grad):
    return (low(grad),)
low.defvjp(low_keep, low_pass)
low_back.defvjp(back_keep, back_low)
EPSILON = 1e-05
ROPE_BASE = 500000.0

def product(left, right):
    return jnp.dot(left, right, precision=lax.Precision.HIGHEST)

def rms_norm(values, gain):
    factor = lax.rsqrt(lax.optimization_barrier(jnp.mean(values * values, axis=-1, keepdims=True)) + EPSILON)
    return values * factor * gain

def rope_tables(position, width):
    half_width = width // 2
    steps_f = jnp.arange(half_width, dtype=jnp.float32)
    inverse = 1.0 / ROPE_BASE ** (steps_f * 2.0 / width)
    angles = position.astype(jnp.float32)[:, None] * inverse[None, :]
    return (jnp.cos(angles)[:, None, :], jnp.sin(angles)[:, None, :])

def rotate(values, cosine_table, sine_table):
    half_width = values.shape[-1] // 2
    first_half = values[..., :half_width]
    second_half = values[..., half_width:]
    return jnp.concatenate([first_half * cosine_table - second_half * sine_table, second_half * cosine_table + first_half * sine_table], axis=-1)

def layout(seq_lengths, seq_group, group_id, row_count):
    owned_mask = (seq_group == group_id).astype(jnp.int32)
    owned_len = seq_lengths * owned_mask
    seq_ends = jnp.cumsum(owned_len).astype(jnp.int32)
    row_index = jnp.arange(row_count, dtype=jnp.int32)
    finished = (seq_ends[None, :] <= row_index[:, None]).astype(jnp.int32)
    segment = lax.optimization_barrier(jnp.sum(finished * owned_mask[None, :], axis=1)).astype(jnp.int32)
    offsets = lax.optimization_barrier(jnp.sum(finished * owned_len[None, :], axis=1)).astype(jnp.int32)
    return (segment, row_index - offsets)

def layer_block(tokens_f, attn_gain, w_query, w_key, w_value, w_out, mlp_gain, w_gate, w_up, w_down, segment, position):
    row_count = tokens_f.shape[0]
    head_group = HEADS // KV_HEADS
    scale = 1.0 / math.sqrt(HEAD_DIM)
    cosine_table, sine_table = rope_tables(position, HEAD_DIM)
    normed = low(rms_norm(tokens_f, attn_gain))
    queries = low(rotate(low_back(product(normed, w_query)).reshape(row_count, HEADS, HEAD_DIM), cosine_table, sine_table))
    keys_all = low(rotate(low_back(product(normed, w_key)).reshape(row_count, KV_HEADS, HEAD_DIM), cosine_table, sine_table))
    values_all = low(low_back(product(normed, w_value))).reshape(row_count, KV_HEADS, HEAD_DIM)
    row_index = jnp.arange(row_count, dtype=jnp.int32)
    allowed = (segment[:, None] == segment[None, :]) & (row_index[None, :] <= row_index[:, None])

    def head_block(operands):
        query_set, key_set, value_set = operands
        scores = low_back(jnp.einsum('gqd,kd->gqk', query_set, key_set, precision=lax.Precision.HIGHEST) * scale)
        weights = jax.nn.softmax(jnp.where(allowed[None], scores, -1e+30), axis=-1)
        return jnp.einsum('gqk,kd->gqd', low(weights), value_set, precision=lax.Precision.HIGHEST)
    grouped = queries.reshape(row_count, KV_HEADS, head_group, HEAD_DIM).transpose(1, 2, 0, 3)
    mixed = lax.map(jax.checkpoint(head_block), (grouped, keys_all.transpose(1, 0, 2), values_all.transpose(1, 0, 2)))
    attended = low(low_back(mixed.transpose(2, 0, 1, 3).reshape(row_count, HEADS * HEAD_DIM)))
    residual = tokens_f + low_back(product(attended, w_out))
    normed_mlp = low(rms_norm(residual, mlp_gain))
    gate = low_back(product(normed_mlp, w_gate))
    up_proj = low_back(product(normed_mlp, w_up))
    hidden = low(jax.nn.silu(gate) * up_proj)
    return residual + product(hidden, w_down)

def reference(tokens, seq_lengths, seq_group, attn_gain, w_query, w_key, w_value, w_out, mlp_gain, w_gate, w_up, w_down, cotangent):
    params = tuple((item.astype(jnp.float32) for item in (attn_gain, w_query, w_key, w_value, w_out, mlp_gain, w_gate, w_up, w_down)))
    row_count = GROUP_TOK

    def per_group(totals, group_id):
        tokens_f = lax.dynamic_slice_in_dim(tokens, group_id * row_count, row_count, 0).astype(jnp.float32)
        incoming = lax.dynamic_slice_in_dim(cotangent, group_id * row_count, row_count, 0).astype(jnp.float32)
        segment, position = layout(seq_lengths, seq_group, group_id, row_count)

        def forward(tokens_in, weights_in):
            return layer_block(tokens_in, weights_in[0], weights_in[1], weights_in[2], weights_in[3], weights_in[4], weights_in[5], weights_in[6], weights_in[7], weights_in[8], segment, position)
        output, pull_back = jax.vjp(forward, tokens_f, params)
        grad_input, grad_params = pull_back(incoming)
        totals = tuple((running + update for running, update in zip(totals, grad_params)))
        return (totals, (output.astype(jnp.bfloat16), grad_input.astype(jnp.bfloat16)))
    start_sums = tuple((jnp.zeros_like(item) for item in params))
    totals, (block_rows, grad_rows) = lax.scan(per_group, start_sums, jnp.arange(N_DP, dtype=jnp.int32))
    return (block_rows.reshape(TOKENS, D), grad_rows.reshape(TOKENS, D), totals[0], totals[1], totals[2], totals[3], totals[4], totals[5], totals[6], totals[7], totals[8])
```

```python
import functools
import math

import jax
import jax.numpy as jnp
from jax import lax
from jax.sharding import PartitionSpec as P

HEAD_DIM = 64
EPSILON = 1e-05
ROPE_BASE = 500000.0
F32 = jnp.float32
BF16 = jnp.bfloat16


def rope_tables(position, width):
    half_width = width // 2
    steps_f = jnp.arange(half_width, dtype=F32)
    inverse = 1.0 / ROPE_BASE ** (steps_f * 2.0 / width)
    angles = position.astype(F32)[:, None] * inverse[None, :]
    return (jnp.cos(angles)[:, None, :], jnp.sin(angles)[:, None, :])


def rotate(values, cosine_table, sine_table):
    half_width = values.shape[-1] // 2
    first_half = values[..., :half_width]
    second_half = values[..., half_width:]
    return jnp.concatenate(
        [
            first_half * cosine_table - second_half * sine_table,
            second_half * cosine_table + first_half * sine_table,
        ],
        axis=-1,
    )


def layout(seq_lengths, seq_group, group_id, place):
    owned_mask = (seq_group == group_id).astype(jnp.int32)
    owned_len = seq_lengths * owned_mask
    seq_ends = jnp.cumsum(owned_len)
    finished = (seq_ends[None, :] <= place[:, None]).astype(jnp.int32)
    segment = jnp.sum(finished * owned_mask[None, :], axis=1)
    offsets = jnp.sum(finished * owned_len[None, :], axis=1)
    return (segment, place - offsets)


def mm(left, right):
    return jnp.dot(left, right, preferred_element_type=F32)


def inner(left, right):
    return lax.dot_general(left, right, (((0,), (0,)), ((), ())), preferred_element_type=F32)


def outer(left, right):
    return lax.dot_general(left, right, (((1,), (1,)), ((), ())), preferred_element_type=F32)


def norm_parts(values):
    factor = lax.rsqrt(jnp.mean(values * values, axis=-1, keepdims=True) + EPSILON)
    return (values * factor, factor)


def norm_back(grad_rows, gain, normed, factor):
    scaled = grad_rows * gain
    return factor * (scaled - normed * jnp.mean(scaled * normed, axis=-1, keepdims=True))


def after(value, *deps):
    return lax.optimization_barrier((value,) + deps)[0]


def add16(*terms):
    return functools.reduce(lambda a, b: a + b, [t.astype(F32) for t in terms]).astype(BF16)


class Line:
    def __init__(self, size):
        self.size = size
        self.index = lax.axis_index("tensor")

    def gather(self, v):
        size = self.size
        left, right = {}, {}
        to_right = to_left = v
        for s in range(1, size):
            to_right = lax.ppermute(to_right, "tensor", [(i, i + 1) for i in range(s - 1, size - 1)])
            to_left = lax.ppermute(to_left, "tensor", [(i, i - 1) for i in range(1, size - s + 1)])
            left[s], right[s] = to_right, to_left
        blocks = [v] + [jnp.where(self.index >= r, left[r], right[size - r]) for r in range(1, size)]
        return jnp.concatenate(blocks, axis=0)

    def scatter(self, parts):
        size = self.size
        from_left = from_right = None
        for s in range(1, size):
            to_right = parts[s] if from_left is None else add16(parts[s], from_left)
            to_left = parts[size - s] if from_right is None else add16(parts[size - s], from_right)
            from_left = lax.ppermute(to_right, "tensor", [(i, i + 1) for i in range(0, s)])
            from_right = lax.ppermute(to_left, "tensor", [(i, i - 1) for i in range(size - s, size)])
        return parts[0].astype(F32) + from_left.astype(F32) + from_right.astype(F32)

    def total(self, v):
        out = v
        for r in range(1, self.size):
            out = out + lax.ppermute(v, "tensor", [(i, (i + r) % self.size) for i in range(self.size)])
        return out


class Cube:
    def __init__(self, size):
        self.size = size
        self.me = lax.axis_index("dp")
        self.bits = [1 << b for b in range(1, size.bit_length() - 1)]
        self.keys = [2 * q for q in range(size // 2)] + [2 * q + 1 for q in range(size // 2)]

    def swap(self, v, m):
        return lax.ppermute(v, "dp", [(i, i ^ m) for i in range(self.size)])

    def gather(self, v, order):
        pieces = {0: v}
        for m in order + [1]:
            pieces.update({k ^ m: self.swap(p, m) for k, p in list(pieces.items())})
        return [pieces[k] for k in self.keys]

    def reduce(self, own, other, axis, order):
        received = self.swap(other, 1)
        width = own.shape[axis] // (self.size // 2)
        pieces = {}
        for q in range(self.size // 2):
            cut = [lax.slice_in_dim(a, q * width, (q + 1) * width, axis=axis) for a in (own, received)]
            pieces[2 * q] = add16(*cut)
        for m in order:
            gone = [k for k in pieces if k & m]
            arrived = {k ^ m: self.swap(pieces.pop(k), m) for k in gone}
            for k, p in arrived.items():
                pieces[k] = (pieces[k].astype(F32) + p.astype(F32)) if m == order[-1] else add16(pieces[k], p)
        return pieces[0]

    def reduce_small(self, v):
        out = v[0]
        for pos, k in enumerate(self.keys):
            if k:
                out = out + self.swap(v[pos], k)
        return out

    def columns_in(self, v):
        width = v.shape[1] // self.size
        return jnp.concatenate(
            [lax.dynamic_slice_in_dim(v, (self.me ^ k) * width, width, 1) for k in self.keys], axis=1
        )

    def columns_out(self, v):
        width = v.shape[1] // self.size
        high = self.size.bit_length() - 2
        blocks = []
        for b in range(self.size):
            k = self.me ^ b
            pos = (k >> 1) | ((k & 1) << high)
            blocks.append(lax.dynamic_slice_in_dim(v, pos * width, width, 1))
        return jnp.concatenate(blocks, axis=1)


def attention_masked(queries, keys_all, segment, place):
    scale = 1.0 / math.sqrt(HEAD_DIM)
    allowed = (segment[:, None] == segment[None, :]) & (place[None, :] <= place[:, None])
    scores = jnp.einsum("qcgd,kcd->cgqk", queries, keys_all, preferred_element_type=F32) * scale
    return jnp.where(allowed, scores, -1e30)


def per_device(
    dp_size,
    tensor_size,
    tokens,
    seq_lengths,
    seq_group,
    attn_gain,
    w_query,
    w_key,
    w_value,
    w_out,
    mlp_gain,
    w_gate,
    w_up,
    w_down,
    cotangent,
):
    cube = Cube(dp_size)
    line = Line(tensor_size)
    order_a, order_b = cube.bits, cube.bits[::-1]
    scale = 1.0 / math.sqrt(HEAD_DIM)
    width_q, width_k = w_query.shape[1], w_key.shape[1]
    own_rows = tokens.shape[0]
    row_count = own_rows * tensor_size
    features = tokens.shape[1]
    half = features // 2

    gains = cube.gather(jnp.stack([attn_gain, mlp_gain]), order_a)
    w_qkv = jnp.concatenate([w_query, w_key, w_value], axis=1)
    cut = w_qkv.shape[0] // 2
    qkv_a = cube.gather(w_qkv[:cut], order_a)
    qkv_b = cube.gather(w_qkv[cut:], order_b)
    tokens_rel = cube.columns_in(tokens)
    rows_all = line.gather(tokens_rel)
    w_out_0, mark = lax.optimization_barrier((w_out, qkv_a[cube.size // 2 - 1]))
    cut = w_out.shape[0] // 2
    out_a = cube.gather(w_out_0[:cut], order_a)
    out_b = cube.gather(w_out_0[cut:], order_b)
    gate_0 = after(w_gate, out_a[cube.size // 2 - 1])
    up_0 = after(w_up, out_a[cube.size // 2 - 1])
    gate_p = cube.gather(gate_0, order_a)
    up_p = cube.gather(up_0, order_b)
    down_0 = after(w_down, gate_p[cube.size // 2 - 1], up_p[cube.size // 2 - 1])
    cut = w_down.shape[0] // 2
    down_a = cube.gather(down_0[:cut], order_a)
    down_b = cube.gather(down_0[cut:], order_b)
    cot_0 = after(cotangent, rows_all)
    cot_rel = cube.columns_in(cot_0)
    incoming = line.gather(cot_rel)

    gain_one = jnp.concatenate([g[0] for g in gains]).astype(F32)
    gain_two = jnp.concatenate([g[1] for g in gains]).astype(F32)
    qkv_w = jnp.concatenate([p for ab in zip(qkv_a, qkv_b) for p in ab], axis=0)
    out_w = jnp.concatenate([jnp.concatenate(out_a, axis=1), jnp.concatenate(out_b, axis=1)], axis=0)
    gate_w = jnp.concatenate(gate_p, axis=0)
    up_w = jnp.concatenate(up_p, axis=0)
    down_w = jnp.concatenate([jnp.concatenate(down_a, axis=1), jnp.concatenate(down_b, axis=1)], axis=0)

    normed_all, _ = norm_parts(rows_all.astype(F32))
    attn_input = (normed_all * gain_one).astype(BF16)
    tokens_f = tokens_rel.astype(F32)
    normed_one, factor_one = norm_parts(tokens_f)
    heads_here = width_q // HEAD_DIM
    kv_here = width_k // HEAD_DIM
    head_group = heads_here // kv_here
    row = jnp.arange(row_count, dtype=jnp.int32)
    owner = lax.rem(line.index - row // own_rows + tensor_size, tensor_size)
    place = owner * own_rows + row % own_rows
    segment, position = layout(seq_lengths, seq_group, cube.me, place)
    cosine_table, sine_table = rope_tables(position, HEAD_DIM)
    qkv = mm(attn_input, qkv_w)
    queries = (
        rotate(qkv[:, :width_q].reshape(row_count, heads_here, HEAD_DIM), cosine_table, sine_table)
        .astype(BF16)
        .reshape(row_count, kv_here, head_group, HEAD_DIM)
    )
    keys_all = rotate(
        qkv[:, width_q : width_q + width_k].reshape(row_count, kv_here, HEAD_DIM), cosine_table, sine_table
    ).astype(BF16)
    values_all = qkv[:, width_q + width_k :].astype(BF16).reshape(row_count, kv_here, HEAD_DIM)
    scores = attention_masked(queries, keys_all, segment, place)
    row_max = jnp.max(scores, axis=-1, keepdims=True)
    exponent = jnp.exp(scores - row_max)
    row_sum = jnp.sum(exponent, axis=-1, keepdims=True)
    weights_low = (exponent / row_sum).astype(BF16)
    mixed = jnp.einsum("cgqk,kcd->qcgd", weights_low, values_all, preferred_element_type=F32)
    attended = mixed.reshape(row_count, heads_here * HEAD_DIM).astype(BF16)
    log_mass = row_max + jnp.log(row_sum)

    def split_rows(v):
        return [lax.slice_in_dim(v, r * own_rows, (r + 1) * own_rows, axis=0) for r in range(tensor_size)]

    residual = tokens_f + line.scatter(split_rows(mm(attended, out_w).astype(BF16)))
    normed_two, factor_two = norm_parts(residual)
    mlp_input = line.gather((normed_two * gain_two).astype(BF16))

    gate = mm(mlp_input, gate_w)
    up_proj = mm(mlp_input, up_w)
    sigmoid_gate = jax.nn.sigmoid(gate)
    hidden = (gate * sigmoid_gate * up_proj).astype(BF16)
    grad_hidden = outer(incoming, down_w)
    silu_slope = sigmoid_gate * (1.0 + gate * (1.0 - sigmoid_gate))
    grad_gate = (grad_hidden * up_proj * silu_slope).astype(BF16)
    grad_up = (grad_hidden * gate * sigmoid_gate).astype(BF16)
    grad_two_parts = (outer(grad_gate, gate_w) + outer(grad_up, up_w)).astype(BF16)
    grad_two = line.scatter(split_rows(grad_two_parts))

    down_grad = cube.reduce(
        inner(hidden, incoming[:, :half]).astype(BF16),
        inner(hidden, incoming[:, half:]).astype(BF16),
        1,
        order_a,
    )
    gate_grad = cube.reduce(
        inner(mlp_input[:, :half], grad_gate).astype(BF16),
        inner(mlp_input[:, half:], grad_gate).astype(BF16),
        0,
        order_b,
    )
    up_grad = cube.reduce(
        inner(mlp_input[:, :half], grad_up).astype(BF16),
        inner(mlp_input[:, half:], grad_up).astype(BF16),
        0,
        order_a,
    )
    block_part = line.scatter(split_rows(mm(hidden, down_w).astype(BF16)))
    block_out = cube.columns_out((residual + block_part).astype(BF16))

    gain_two_part = jnp.sum(grad_two * normed_two, axis=0)
    grad_residual = cot_rel.astype(F32) + norm_back(grad_two, gain_two, normed_two, factor_two)
    grad_attn_rows = line.gather(grad_residual.astype(BF16))

    grad_attended = outer(grad_attn_rows, out_w).astype(BF16)
    grad_block = grad_attended.reshape(row_count, kv_here, head_group, HEAD_DIM)
    scores = attention_masked(queries, keys_all, segment, place)
    probs = jnp.exp(scores - log_mass)
    weights_low = probs.astype(BF16)
    grad_probs = jnp.einsum("qcgd,kcd->cgqk", grad_block, values_all, preferred_element_type=F32)
    delta = jnp.sum(probs * grad_probs, axis=-1, keepdims=True)
    grad_scores = (probs * (grad_probs - delta)).astype(BF16)
    grad_queries = jnp.einsum("cgqk,kcd->qcgd", grad_scores, keys_all, preferred_element_type=F32) * scale
    grad_keys = jnp.einsum("cgqk,qcgd->kcd", grad_scores, queries, preferred_element_type=F32) * scale
    grad_values = jnp.einsum("cgqk,qcgd->kcd", weights_low, grad_block, preferred_element_type=F32)
    grad_queries = (
        rotate(grad_queries.reshape(row_count, heads_here, HEAD_DIM), cosine_table, -sine_table)
        .astype(BF16)
        .reshape(row_count, width_q)
    )
    grad_keys = rotate(grad_keys, cosine_table, -sine_table).astype(BF16).reshape(row_count, width_k)
    grad_qkv = jnp.concatenate(
        [grad_queries, grad_keys, grad_values.astype(BF16).reshape(row_count, width_k)], axis=1
    )
    grad_one_parts = outer(grad_qkv, qkv_w)
    gain_one_part = jnp.sum(grad_one_parts * normed_all, axis=0)
    grad_one = line.scatter(split_rows(grad_one_parts.astype(BF16)))
    qkv_grad = cube.reduce(
        inner(attn_input[:, :half], grad_qkv).astype(BF16),
        inner(attn_input[:, half:], grad_qkv).astype(BF16),
        0,
        order_b,
    )
    out_grad = cube.reduce(
        inner(attended, grad_attn_rows[:, :half]).astype(BF16),
        inner(attended, grad_attn_rows[:, half:]).astype(BF16),
        1,
        order_a,
    )
    gain_two_sum = cube.reduce_small(line.total(gain_two_part).reshape(dp_size, 1, -1))
    gain_one_sum = cube.reduce_small(line.total(gain_one_part).reshape(dp_size, 1, -1))
    grad_tokens = cube.columns_out(
        (grad_residual + norm_back(grad_one, gain_one, normed_one, factor_one)).astype(BF16)
    )
    return (
        block_out,
        grad_tokens,
        gain_one_sum[0],
        qkv_grad[:, :width_q],
        qkv_grad[:, width_q : width_q + width_k],
        qkv_grad[:, width_q + width_k :],
        out_grad,
        gain_two_sum[0],
        gate_grad,
        up_grad,
        down_grad,
    )


def solution(mesh):
    return jax.shard_map(
        functools.partial(per_device, mesh.shape["dp"], mesh.shape["tensor"]),
        mesh=mesh,
        in_specs=(
            P(("dp", "tensor"), None),
            P(),
            P(),
            P("dp"),
            P("dp", "tensor"),
            P("dp", "tensor"),
            P("dp", "tensor"),
            P("tensor", "dp"),
            P("dp"),
            P("dp", "tensor"),
            P("dp", "tensor"),
            P("tensor", "dp"),
            P(("dp", "tensor"), None),
        ),
        out_specs=(
            P(("dp", "tensor"), None),
            P(("dp", "tensor"), None),
            P("dp"),
            P("dp", "tensor"),
            P("dp", "tensor"),
            P("dp", "tensor"),
            P("tensor", "dp"),
            P("dp"),
            P("dp", "tensor"),
            P("dp", "tensor"),
            P("tensor", "dp"),
        ),
        check_vma=False,
    )
```

```python
import functools
import math

import jax
import jax.numpy as jnp
from jax import lax
from jax.experimental import pallas as pl
from jax.experimental.pallas import tpu as pltpu
from jax.sharding import PartitionSpec as P

HEAD_DIM = 64
EPSILON = 1e-05
ROPE_BASE = 500000.0
F32 = jnp.float32
BF16 = jnp.bfloat16


def rope_tables(position, width):
    half_width = width // 2
    steps_f = jnp.arange(half_width, dtype=F32)
    inverse = 1.0 / ROPE_BASE ** (steps_f * 2.0 / width)
    angles = position.astype(F32)[:, None] * inverse[None, :]
    return (jnp.cos(angles)[:, None, :], jnp.sin(angles)[:, None, :])


def rotate(values, cosine_table, sine_table):
    half_width = values.shape[-1] // 2
    first_half = values[..., :half_width]
    second_half = values[..., half_width:]
    return jnp.concatenate(
        [
            first_half * cosine_table - second_half * sine_table,
            second_half * cosine_table + first_half * sine_table,
        ],
        axis=-1,
    )


def layout(seq_lengths, seq_group, group_id, place):
    owned_mask = (seq_group == group_id).astype(jnp.int32)
    owned_len = seq_lengths * owned_mask
    seq_ends = jnp.cumsum(owned_len)
    finished = (seq_ends[None, :] <= place[:, None]).astype(jnp.int32)
    segment = jnp.sum(finished * owned_mask[None, :], axis=1)
    offsets = jnp.sum(finished * owned_len[None, :], axis=1)
    return (segment, place - offsets)


def mm(left, right):
    return jnp.dot(left, right, preferred_element_type=F32)


def inner(left, right):
    return lax.dot_general(left, right, (((0,), (0,)), ((), ())), preferred_element_type=F32)


def outer(left, right):
    return lax.dot_general(left, right, (((1,), (1,)), ((), ())), preferred_element_type=F32)


def norm_parts(values):
    factor = lax.rsqrt(jnp.mean(values * values, axis=-1, keepdims=True) + EPSILON)
    return (values * factor, factor)


def norm_back(grad_rows, gain, normed, factor):
    scaled = grad_rows * gain
    return factor * (scaled - normed * jnp.mean(scaled * normed, axis=-1, keepdims=True))


def after(value, *deps):
    return lax.optimization_barrier((value,) + deps)[0]


class Line:
    def __init__(self, size):
        self.size = size
        self.index = lax.axis_index("tensor")

    def shift(self, v, r):
        return lax.ppermute(v, "tensor", [(i, (i + r) % self.size) for i in range(self.size)])

    def gather(self, v):
        return [v] + [self.shift(v, r) for r in range(1, self.size)]

    def scatter(self, parts):
        return [parts[0]] + [self.shift(parts[r], -r) for r in range(1, self.size)]

    def total(self, v):
        return functools.reduce(lambda a, b: a + b, [v] + [self.shift(v, r) for r in range(1, self.size)])


class Cube:
    def __init__(self, size):
        self.size = size
        self.me = lax.axis_index("dp")
        self.bits = [1 << b for b in range(size.bit_length() - 1)]
        self.keys = [2 * q for q in range(size // 2)] + [2 * q + 1 for q in range(size // 2)]

    def swap(self, v, m):
        return lax.ppermute(v, "dp", [(i, i ^ m) for i in range(self.size)])

    def gather_row(self, v):
        width = v.shape[1]
        for m in self.bits:
            v = jnp.concatenate([v, self.swap(v, m)], axis=1)
        cuts = [lax.dynamic_slice_in_dim(v, (self.me ^ b) * width, width, 1) for b in range(self.size)]
        return jnp.concatenate(cuts, axis=1)

    def places(self):
        return 2 * jnp.arange(self.size // 2, dtype=jnp.int32) + (self.me & 1)

    def over_chips(self, own):
        groups = [list(range(c, self.size, 2)) for c in range(2)]
        return lax.psum_scatter(own, "dp", scatter_dimension=0, axis_index_groups=groups, tiled=True)


class Order:
    def __init__(self):
        self.last = None

    def __call__(self, step, *args):
        if self.last is not None:
            args, _ = lax.optimization_barrier((args, self.last))
        out = step(*args)
        self.last = jax.tree.leaves(out)[0]
        return out


def total32(terms):
    return functools.reduce(lambda a, b: a + b, [t.astype(F32) for t in terms])


def tile_of(size, most):
    while size % most:
        most //= 2
    return most


def kernel_call(body, name, flops, operands, out_shape, vmem=48, **kwargs):
    shapes = jax.tree.leaves(out_shape)
    moved = sum(math.prod(a.shape) * a.dtype.itemsize for a in list(operands) + shapes)
    return pl.pallas_call(
        body,
        out_shape=out_shape,
        name=name,
        cost_estimate=pl.CostEstimate(flops=flops, bytes_accessed=moved, transcendentals=0),
        compiler_params=pltpu.CompilerParams(vmem_limit_bytes=vmem << 20),
        **kwargs,
    )(*operands)


def whole(shape):
    return pl.BlockSpec(shape, lambda *_: (0,) * len(shape))


def attention_in(x_blocks, gain, w, skip):
    count = len(x_blocks)
    rows, features = x_blocks[0].shape
    total, width = rows * count, w.shape[1] - skip
    tile = math.gcd(math.gcd(width, skip), 256)

    def body(*refs):
        x_refs, (gain_ref, w_ref, h_ref, out_ref) = refs[:count], refs[count:]

        @pl.when(pl.program_id(0) == 0)
        def _():
            for r in range(count):
                normed, _ = norm_parts(x_refs[r][...].astype(F32))
                h_ref[r * rows : (r + 1) * rows, :] = (normed * gain_ref[...]).astype(BF16)

        out_ref[...] = mm(h_ref[...], w_ref[...])

    return kernel_call(
        body,
        "attention_in",
        2 * total * features * width,
        (*x_blocks, gain, w),
        (jax.ShapeDtypeStruct((total, features), BF16), jax.ShapeDtypeStruct((total, width), F32)),
        grid=(width // tile,),
        in_specs=[whole((rows, features))] * count
        + [whole((1, features)), pl.BlockSpec((features, tile), lambda j: (0, skip // tile + j))],
        out_specs=[whole((total, features)), pl.BlockSpec((total, tile), lambda j: (0, j))],
    )


def feed_forward(h_blocks, c, w):
    count = len(h_blocks)
    rows, features = h_blocks[0].shape
    units = w.shape[1] // 3
    tile = tile_of(units, 256)
    steps = units // tile

    def body(*refs):
        h_refs = refs[:count]
        c_ref, gate_ref, up_ref, down_ref, h_all, out_ref = refs[count:]

        @pl.when(pl.program_id(0) == 0)
        def _():
            for r in range(count):
                h_all[r * rows : (r + 1) * rows, :] = h_refs[r][...]

        gate = mm(h_all[...], gate_ref[...])
        up = mm(h_all[...], up_ref[...])
        grad_hidden = mm(c_ref[...], down_ref[...])
        sig = 1.0 / (1.0 + jnp.exp(-gate))
        silu = gate * sig
        out_ref[0] = (grad_hidden * up * (sig * (1.0 + gate * (1.0 - sig)))).astype(BF16)
        out_ref[1] = (grad_hidden * silu).astype(BF16)
        out_ref[2] = (silu * up).astype(BF16)

    total = rows * count
    return kernel_call(
        body,
        "feed_forward",
        6 * total * features * units,
        (*h_blocks, c, w, w, w),
        (jax.ShapeDtypeStruct((total, features), BF16), jax.ShapeDtypeStruct((3, total, units), BF16)),
        grid=(steps,),
        in_specs=[whole((rows, features))] * count
        + [whole((total, features))]
        + [pl.BlockSpec((features, tile), lambda j, k=k: (0, k * steps + j)) for k in range(3)],
        out_specs=[whole((total, features)), pl.BlockSpec((3, total, tile), lambda j: (0, 0, j))],
    )


def rows_product(a, leads, w, first, count, name):
    rows, units = a.shape[1:]
    features = w.shape[0]
    tile = tile_of(features, 256)
    block = rows // count
    width = units * len(leads)
    aligned = first % width == 0

    def body(*refs):
        a_refs, w_ref, outs = refs[: len(leads)], refs[len(leads)], refs[len(leads) + 1 :]
        at = 0 if aligned else first
        acc = None
        for a_ref in a_refs:
            term = outer(a_ref[0], w_ref[:, at : at + units])
            acc = term if acc is None else acc + term
            at += units
        for r in range(count):
            outs[r][...] = acc[r * block : (r + 1) * block, :].astype(BF16)

    spec = pl.BlockSpec((tile, width), lambda j: (j, first // width))
    if not aligned:
        spec = pl.BlockSpec((tile, w.shape[1]), lambda j: (j, 0))
    return kernel_call(
        body,
        name,
        2 * rows * features * width,
        [a] * len(leads) + [w],
        [jax.ShapeDtypeStruct((block, features), BF16)] * count,
        grid=(features // tile,),
        in_specs=[pl.BlockSpec((1, rows, units), lambda j, k=k: (k, 0, 0)) for k in leads] + [spec],
        out_specs=[pl.BlockSpec((block, tile), lambda j: (0, j))] * count,
    )


def weight_grad(sides, parts, places, pieces, most, name):
    terms = len(sides[0])
    rows, width = sides[0][0].shape[0], sides[0][0].shape[1] // pieces
    count = places.shape[0]
    sizes = [n[0][0].shape[-1] for _, n in parts]
    tile = functools.reduce(math.gcd, sizes, most)
    starts = [0]
    for size in sizes:
        starts.append(starts[-1] + size // tile)
    n_sides, n_parts = len(sides), len(parts)

    def body(places_ref, *refs):
        d_refs = refs[: n_sides * terms * count]
        n_refs = refs[n_sides * terms * count :][: n_parts * terms]
        out_ref, turned = refs[-2:]
        j = pl.program_id(0)

        @pl.when(j == 0)
        def _():
            for k in range(n_sides * terms):
                for q in range(count):
                    turned[k, q * width : (q + 1) * width, :] = d_refs[k * count + q][...].T

        for p, (side, _) in enumerate(parts):

            @pl.when((j >= starts[p]) & (j < starts[p + 1]))
            def _(p=p, side=side):
                acc = None
                for t in range(terms):
                    term = mm(turned[side * terms + t], n_refs[p * terms + t][0])
                    acc = term if acc is None else acc + term
                out_ref[...] = acc.astype(BF16)

    def n_spec(p, lead):
        last = starts[p + 1] - starts[p] - 1
        return pl.BlockSpec((1, rows, tile), lambda j, _: (lead, 0, jnp.clip(j - starts[p], 0, last)))

    in_specs = [
        pl.BlockSpec((rows, width), lambda j, p, q=q: (0, p[q])) for _ in range(n_sides * terms) for q in range(count)
    ]
    in_specs += [n_spec(p, lead) for p, (_, n) in enumerate(parts) for _, lead in n]
    operands = [places] + [d for side in sides for d in side for _ in range(count)]
    operands += [a for _, n in parts for a, _ in n]
    return kernel_call(
        body,
        name,
        2 * terms * rows * count * width * starts[-1] * tile,
        operands,
        jax.ShapeDtypeStruct((count * width, starts[-1] * tile), BF16),
        grid_spec=pltpu.PrefetchScalarGridSpec(
            num_scalar_prefetch=1,
            grid=(starts[-1],),
            in_specs=in_specs,
            out_specs=pl.BlockSpec((count * width, tile), lambda j, _: (0, j)),
            scratch_shapes=[pltpu.VMEM((n_sides * terms, count * width, rows), BF16)],
        ),
    )


def attention_masked(queries, keys_all, segment, place):
    scale = 1.0 / math.sqrt(HEAD_DIM)
    allowed = (segment[:, None] == segment[None, :]) & (place[None, :] <= place[:, None])
    scores = jnp.einsum("qcgd,kcd->cgqk", queries, keys_all, preferred_element_type=F32) * scale
    return jnp.where(allowed, scores, -1e30)


def per_device(
    dp_size,
    tensor_size,
    tokens,
    seq_lengths,
    seq_group,
    attn_gain,
    w_query,
    w_key,
    w_value,
    w_out,
    mlp_gain,
    w_gate,
    w_up,
    w_down,
    cotangent,
):
    cube = Cube(dp_size)
    line = Line(tensor_size)
    scale = 1.0 / math.sqrt(HEAD_DIM)
    width_q, width_k = w_query.shape[1], w_key.shape[1]
    own_rows = tokens.shape[0]
    row_count = own_rows * tensor_size

    width_out, units = w_out.shape[0], w_gate.shape[1]

    rows_all = line.gather(tokens)
    gain_one = cube.gather_row(attn_gain[None, :]).astype(F32)
    w_attn = lax.all_gather(jnp.concatenate([w_out.T, w_query, w_key, w_value], axis=1), "dp", axis=0, tiled=True)
    gain_two = cube.gather_row(mlp_gain[None, :]).astype(F32)
    w_mlp = lax.all_gather(jnp.concatenate([w_gate, w_up, w_down.T], axis=1), "dp", axis=0, tiled=True)
    incoming = jnp.concatenate(line.gather(after(cotangent, *rows_all)), axis=0)
    incoming_other = cube.swap(incoming, 1)

    order = Order()
    attn_input, qkv = order(lambda *a: attention_in(a[:-2], a[-2], a[-1], width_out), *rows_all, gain_one, w_attn)
    tokens_f = tokens.astype(F32)
    normed_one, factor_one = norm_parts(tokens_f)
    heads_here = width_q // HEAD_DIM
    kv_here = width_k // HEAD_DIM
    head_group = heads_here // kv_here
    row = jnp.arange(row_count, dtype=jnp.int32)
    owner = lax.rem(line.index - row // own_rows + tensor_size, tensor_size)
    place = owner * own_rows + row % own_rows
    segment, position = layout(seq_lengths, seq_group, cube.me, place)
    cosine_table, sine_table = rope_tables(position, HEAD_DIM)
    queries = (
        rotate(qkv[:, :width_q].reshape(row_count, heads_here, HEAD_DIM), cosine_table, sine_table)
        .astype(BF16)
        .reshape(row_count, kv_here, head_group, HEAD_DIM)
    )
    keys_all = rotate(
        qkv[:, width_q : width_q + width_k].reshape(row_count, kv_here, HEAD_DIM), cosine_table, sine_table
    ).astype(BF16)
    values_all = qkv[:, width_q + width_k :].astype(BF16).reshape(row_count, kv_here, HEAD_DIM)
    scores = attention_masked(queries, keys_all, segment, place)
    row_max = jnp.max(scores, axis=-1, keepdims=True)
    exponent = jnp.exp(scores - row_max)
    row_sum = jnp.sum(exponent, axis=-1, keepdims=True)
    weights_low = (exponent / row_sum).astype(BF16)
    mixed = jnp.einsum("cgqk,kcd->qcgd", weights_low, values_all, preferred_element_type=F32)
    attended = mixed.reshape(row_count, heads_here * HEAD_DIM).astype(BF16)
    log_mass = row_max + jnp.log(row_sum)

    out_parts = order(
        lambda a, w: rows_product(a, [0], w, 0, tensor_size, "attention_out"), attended[None], w_attn
    )
    residual = order(lambda x, *terms: x + total32(terms), tokens_f, *line.scatter(out_parts))
    normed_two, factor_two = norm_parts(residual)
    mlp_blocks = line.gather((normed_two * gain_two).astype(BF16))

    mlp_input, unit_grads = order(feed_forward, mlp_blocks, incoming, w_mlp)
    mlp_input_other, unit_grads_other = cube.swap(mlp_input, 1), cube.swap(unit_grads, 1)
    two_parts = order(
        lambda a, w: rows_product(a, [0, 1], w, 0, tensor_size, "feed_forward_rows_grad"), unit_grads, w_mlp
    )
    two_terms = line.scatter(two_parts)

    def mlp_grad(h, h_other, c, c_other, n, n_other):
        parts = [(side, [(n, lead), (n_other, lead)]) for side, lead in ((0, 0), (0, 1), (1, 2))]
        sides = [[h, h_other], [c, c_other]]
        return weight_grad(sides, parts, cube.places(), dp_size, 512, "feed_forward_grad")

    mlp_sum = cube.over_chips(
        order(mlp_grad, mlp_input, mlp_input_other, incoming, incoming_other, unit_grads, unit_grads_other)
    )

    grad_residual = order(
        lambda c, g, n, f, *terms: c.astype(F32) + norm_back(total32(terms), g, n, f),
        cotangent,
        gain_two,
        normed_two,
        factor_two,
        *two_terms,
    )
    gathered = line.gather(grad_residual.astype(BF16))
    block_parts = order(
        lambda a, w: rows_product(a, [2], w, 2 * units, tensor_size, "block_out"), unit_grads, w_mlp
    )
    grad_attn_rows = order(lambda *b: jnp.concatenate(b, axis=0), *gathered)
    block_terms = line.scatter(lax.optimization_barrier((block_parts, grad_attn_rows))[0])

    grad_attended = mm(grad_attn_rows, w_attn[:, :width_out]).astype(BF16)
    grad_block = grad_attended.reshape(row_count, kv_here, head_group, HEAD_DIM)
    scores = attention_masked(queries, keys_all, segment, place)
    probs = jnp.exp(scores - log_mass)
    weights_low = probs.astype(BF16)
    grad_probs = jnp.einsum("qcgd,kcd->cgqk", grad_block, values_all, preferred_element_type=F32)
    delta = jnp.sum(probs * grad_probs, axis=-1, keepdims=True)
    grad_scores = (probs * (grad_probs - delta)).astype(BF16)
    grad_queries = jnp.einsum("cgqk,kcd->qcgd", grad_scores, keys_all, preferred_element_type=F32) * scale
    grad_keys = jnp.einsum("cgqk,qcgd->kcd", grad_scores, queries, preferred_element_type=F32) * scale
    grad_values = jnp.einsum("cgqk,qcgd->kcd", weights_low, grad_block, preferred_element_type=F32)
    grad_queries = (
        rotate(grad_queries.reshape(row_count, heads_here, HEAD_DIM), cosine_table, -sine_table)
        .astype(BF16)
        .reshape(row_count, width_q)
    )
    grad_keys = rotate(grad_keys, cosine_table, -sine_table).astype(BF16).reshape(row_count, width_k)
    grad_qkv = jnp.concatenate(
        [grad_queries, grad_keys, grad_values.astype(BF16).reshape(row_count, width_k)], axis=1
    )
    one_parts = order(
        lambda a, w: rows_product(a, [0], w, width_out, tensor_size, "attention_rows_grad"),
        after(grad_qkv, *block_terms)[None],
        w_attn,
    )
    one_terms = line.scatter(one_parts)

    def attn_grad(y, h, a, g):
        parts = [(0, [(a[None], 0)]), (1, [(g[None], 0)])]
        places = jnp.arange(dp_size, dtype=jnp.int32)
        return weight_grad([[y], [h]], parts, places, dp_size, 256, "attention_grad")

    attn_terms = order(attn_grad, grad_attn_rows, attn_input, attended, grad_qkv)
    attn_sum = lax.psum_scatter(after(attn_terms, mlp_sum), "dp", scatter_dimension=0, tiled=True)
    mlp_sum = mlp_sum.astype(F32)
    gate_grad, up_grad, down_grad = mlp_sum[:, :units], mlp_sum[:, units : 2 * units], mlp_sum[:, 2 * units :].T
    block_out = (residual + total32(block_terms)).astype(BF16)
    attn_sum = attn_sum.astype(F32)
    out_grad, qkv_grad = attn_sum[:, :width_out].T, attn_sum[:, width_out:]
    query_grad = qkv_grad[:, :width_q]
    key_grad = qkv_grad[:, width_q : width_q + width_k]
    value_grad = qkv_grad[:, width_q + width_k :]

    def gain_terms(*pairs):
        return functools.reduce(lambda a, b: a + b, [jnp.sum(w.astype(F32) * g, axis=1) for w, g in pairs])

    gain_sums = line.total(
        jnp.stack(
            [
                gain_terms((w_query, query_grad), (w_key, key_grad), (w_value, value_grad)),
                gain_terms((w_gate, gate_grad), (w_up, up_grad)),
            ]
        )
    )
    attn_gain_grad = gain_sums[0] / attn_gain.astype(F32)
    mlp_gain_grad = gain_sums[1] / mlp_gain.astype(F32)
    grad_tokens = order(
        lambda c, g, n, f, *terms: (c + norm_back(total32(terms), g, n, f)).astype(BF16),
        grad_residual,
        gain_one,
        normed_one,
        factor_one,
        *one_terms,
    )
    return (
        block_out,
        grad_tokens,
        attn_gain_grad,
        query_grad,
        key_grad,
        value_grad,
        out_grad,
        mlp_gain_grad,
        gate_grad,
        up_grad,
        down_grad,
    )


def solution(mesh):
    return jax.shard_map(
        functools.partial(per_device, mesh.shape["dp"], mesh.shape["tensor"]),
        mesh=mesh,
        in_specs=(
            P(("dp", "tensor"), None),
            P(),
            P(),
            P("dp"),
            P("dp", "tensor"),
            P("dp", "tensor"),
            P("dp", "tensor"),
            P("tensor", "dp"),
            P("dp"),
            P("dp", "tensor"),
            P("dp", "tensor"),
            P("tensor", "dp"),
            P(("dp", "tensor"), None),
        ),
        out_specs=(
            P(("dp", "tensor"), None),
            P(("dp", "tensor"), None),
            P("dp"),
            P("dp", "tensor"),
            P("dp", "tensor"),
            P("dp", "tensor"),
            P("tensor", "dp"),
            P("dp"),
            P("dp", "tensor"),
            P("dp", "tensor"),
            P("tensor", "dp"),
        ),
        check_vma=False,
    )
```

```python
import functools
import math

import jax
import jax.numpy as jnp
from jax import lax
from jax.experimental import pallas as pl
from jax.experimental.pallas import tpu as pltpu
from jax.sharding import PartitionSpec as P

HEAD_DIM = 64
EPSILON = 1e-05
ROPE_BASE = 500000.0
F32 = jnp.float32
BF16 = jnp.bfloat16


def rope_tables(position, width):
    half_width = width // 2
    steps_f = jnp.arange(half_width, dtype=F32)
    inverse = 1.0 / ROPE_BASE ** (steps_f * 2.0 / width)
    angles = position.astype(F32)[:, None] * inverse[None, :]
    return (jnp.cos(angles)[:, None, :], jnp.sin(angles)[:, None, :])


def rotate(values, cosine_table, sine_table):
    half_width = values.shape[-1] // 2
    first_half = values[..., :half_width]
    second_half = values[..., half_width:]
    return jnp.concatenate(
        [
            first_half * cosine_table - second_half * sine_table,
            second_half * cosine_table + first_half * sine_table,
        ],
        axis=-1,
    )


def layout(seq_lengths, seq_group, group_id, place):
    owned_mask = (seq_group == group_id).astype(jnp.int32)
    owned_len = seq_lengths * owned_mask
    seq_ends = jnp.cumsum(owned_len)
    finished = (seq_ends[None, :] <= place[:, None]).astype(jnp.int32)
    segment = jnp.sum(finished * owned_mask[None, :], axis=1)
    offsets = jnp.sum(finished * owned_len[None, :], axis=1)
    return (segment, place - offsets)


def mm(left, right):
    return jnp.dot(left, right, preferred_element_type=F32)


def inner(left, right):
    return lax.dot_general(left, right, (((0,), (0,)), ((), ())), preferred_element_type=F32)


def outer(left, right):
    return lax.dot_general(left, right, (((1,), (1,)), ((), ())), preferred_element_type=F32)


def norm_parts(values):
    factor = lax.rsqrt(jnp.mean(values * values, axis=-1, keepdims=True) + EPSILON)
    return (values * factor, factor)


def norm_back(grad_rows, gain, normed, factor):
    scaled = grad_rows * gain
    return factor * (scaled - normed * jnp.mean(scaled * normed, axis=-1, keepdims=True))


def after(value, *deps):
    return lax.optimization_barrier((value,) + deps)[0]


class Line:
    def __init__(self, size):
        self.size = size
        self.index = lax.axis_index("tensor")
        self.owners = lax.rem(self.index - jnp.arange(size, dtype=jnp.int32) + size, size)

    def shift(self, v, r):
        return lax.ppermute(v, "tensor", [(i, (i + r) % self.size) for i in range(self.size)])

    def gather(self, v):
        return [v] + [self.shift(v, r) for r in range(1, self.size)]

    def scatter(self, parts):
        return [parts[0]] + [self.shift(parts[r], -r) for r in range(1, self.size)]

    def total(self, v):
        return functools.reduce(lambda a, b: a + b, [v] + [self.shift(v, r) for r in range(1, self.size)])


class Cube:
    def __init__(self, size):
        self.size = size
        self.me = lax.axis_index("dp")
        self.bits = [1 << b for b in range(size.bit_length() - 1)]

    def swap(self, v, m):
        return lax.ppermute(v, "dp", [(i, i ^ m) for i in range(self.size)])

    def gather_columns(self, v):
        for m in self.bits:
            other = self.swap(v, m)
            both = jnp.concatenate([v, other], axis=1), jnp.concatenate([other, v], axis=1)
            v = jnp.where((self.me & m) == 0, *both)
        return v

    def places(self, half):
        count = self.size // 2
        bits = self.hops(half)
        keys = [0]
        for m in reversed(bits):
            keys = keys + [k | m for k in keys]
        return self.me ^ jnp.array(keys[:count], jnp.int32)

    def hops(self, half):
        return self.bits[1:] if half else self.bits[:0:-1]

    def first_hop(self, pairs):
        return [(keep, self.swap(send, self.hops(half)[0])) for half, (keep, send) in enumerate(pairs)]

    def other_hops(self, pairs, order):
        pairs = list(pairs)
        for hop in range(1, len(self.bits) - 1):
            totals = order(lambda *p: [total32(terms).astype(BF16) for terms in p], *pairs)
            cut = totals[0].shape[0] // 2
            pairs = [(t[:cut], self.swap(t[cut:], self.hops(half)[hop])) for half, t in enumerate(totals)]
        return pairs


class Order:
    def __init__(self):
        self.last = None

    def __call__(self, step, *args):
        if self.last is not None:
            args, _ = lax.optimization_barrier((args, self.last))
        out = step(*args)
        self.last = jax.tree.leaves(out)[0]
        return out


def total32(terms):
    return functools.reduce(lambda a, b: a + b, [t.astype(F32) for t in terms])


def tile_of(size, most):
    while size % most:
        most //= 2
    return most


def kernel_call(body, name, flops, operands, out_shape, vmem=48, **kwargs):
    shapes = jax.tree.leaves(out_shape)
    moved = sum(math.prod(a.shape) * a.dtype.itemsize for a in list(operands) + shapes)
    return pl.pallas_call(
        body,
        out_shape=out_shape,
        name=name,
        cost_estimate=pl.CostEstimate(flops=flops, bytes_accessed=moved, transcendentals=0),
        compiler_params=pltpu.CompilerParams(vmem_limit_bytes=vmem << 20),
        **kwargs,
    )(*operands)


def whole(shape):
    return pl.BlockSpec(shape, lambda *_: (0,) * len(shape))


def attention_in(x_blocks, gain, w, skip, owners):
    count = len(x_blocks)
    rows, features = x_blocks[0].shape
    total, width = rows * count, w.shape[1] - skip
    tile = math.gcd(math.gcd(width, skip), 256)

    def body(owners_ref, *refs):
        x_refs, (gain_ref, w_ref, h_ref, out_ref) = refs[:count], refs[count:]

        @pl.when(pl.program_id(0) == 0)
        def _():
            for r in range(count):
                normed, _ = norm_parts(x_refs[r][...].astype(F32))
                at = pl.multiple_of(owners_ref[r] * rows, rows)
                h_ref[pl.ds(at, rows), :] = (normed * gain_ref[...]).astype(BF16)

        out_ref[...] = mm(h_ref[...], w_ref[...])

    return kernel_call(
        body,
        "attention_in",
        2 * total * features * width,
        (owners, *x_blocks, gain, w),
        (jax.ShapeDtypeStruct((total, features), BF16), jax.ShapeDtypeStruct((total, width), F32)),
        grid_spec=pltpu.PrefetchScalarGridSpec(
            num_scalar_prefetch=1,
            grid=(width // tile,),
            in_specs=[whole((rows, features))] * count
            + [whole((1, features)), pl.BlockSpec((features, tile), lambda j, _: (0, skip // tile + j))],
            out_specs=[whole((total, features)), pl.BlockSpec((total, tile), lambda j, _: (0, j))],
        ),
    )


def feed_forward(h_blocks, c_blocks, w, owners):
    count = len(h_blocks)
    rows, features = h_blocks[0].shape
    units = w.shape[1] // 3
    tile = tile_of(units, 256)
    steps = units // tile

    def body(owners_ref, *refs):
        h_refs, c_refs = refs[:count], refs[count : 2 * count]
        gate_ref, up_ref, down_ref, h_all, c_all, out_ref = refs[2 * count :]

        @pl.when(pl.program_id(0) == 0)
        def _():
            for r in range(count):
                at = pl.multiple_of(owners_ref[r] * rows, rows)
                h_all[pl.ds(at, rows), :] = h_refs[r][...]
                c_all[pl.ds(at, rows), :] = c_refs[r][...]

        gate = mm(h_all[...], gate_ref[...])
        up = mm(h_all[...], up_ref[...])
        grad_hidden = mm(c_all[...], down_ref[...])
        sig = 1.0 / (1.0 + jnp.exp(-gate))
        silu = gate * sig
        out_ref[0] = (grad_hidden * up * (sig * (1.0 + gate * (1.0 - sig)))).astype(BF16)
        out_ref[1] = (grad_hidden * silu).astype(BF16)
        out_ref[2] = (silu * up).astype(BF16)

    total = rows * count
    wide = jax.ShapeDtypeStruct((total, features), BF16)
    return kernel_call(
        body,
        "feed_forward",
        6 * total * features * units,
        (owners, *h_blocks, *c_blocks, w, w, w),
        (wide, wide, jax.ShapeDtypeStruct((3, total, units), BF16)),
        grid_spec=pltpu.PrefetchScalarGridSpec(
            num_scalar_prefetch=1,
            grid=(steps,),
            in_specs=[whole((rows, features))] * (2 * count)
            + [pl.BlockSpec((features, tile), lambda j, _, k=k: (0, k * steps + j)) for k in range(3)],
            out_specs=[whole((total, features))] * 2 + [pl.BlockSpec((3, total, tile), lambda j, _: (0, 0, j))],
        ),
    )


def rows_product(a, leads, w, first, name, owners=None):
    rows, units = a.shape[1:]
    features = w.shape[0]
    tile = tile_of(features, 256)
    count = 1 if owners is None else owners.shape[0]
    block = rows // count
    width = units * len(leads)
    aligned = first % width == 0

    def body(owners_ref, *refs):
        a_refs, w_ref, outs, turned = refs[: len(leads)], refs[len(leads)], refs[len(leads) + 1 : -1], refs[-1]
        if owners is not None:

            @pl.when(pl.program_id(0) == 0)
            def _():
                for r in range(count):
                    at = pl.multiple_of(owners_ref[r] * block, block)
                    for k in range(len(leads)):
                        turned[k, r * block : (r + 1) * block, :] = a_refs[k][0, pl.ds(at, block), :]

        at = 0 if aligned else first
        acc = None
        for k, a_ref in enumerate(a_refs):
            term = outer(a_ref[0] if owners is None else turned[k], w_ref[:, at : at + units])
            acc = term if acc is None else acc + term
            at += units
        for r in range(count):
            outs[r][...] = acc[r * block : (r + 1) * block, :].astype(BF16)

    spec = pl.BlockSpec((tile, width), lambda j, _: (j, first // width))
    if not aligned:
        spec = pl.BlockSpec((tile, w.shape[1]), lambda j, _: (j, 0))
    outs = kernel_call(
        body,
        name,
        2 * rows * features * width,
        [jnp.zeros((1,), jnp.int32) if owners is None else owners] + [a] * len(leads) + [w],
        [jax.ShapeDtypeStruct((block, features), BF16)] * count,
        grid_spec=pltpu.PrefetchScalarGridSpec(
            num_scalar_prefetch=1,
            grid=(features // tile,),
            in_specs=[pl.BlockSpec((1, rows, units), lambda j, _, k=k: (k, 0, 0)) for k in leads] + [spec],
            out_specs=[pl.BlockSpec((block, tile), lambda j, _: (0, j))] * count,
            scratch_shapes=[pltpu.VMEM((len(leads), rows, units) if owners is not None else (1, 16, 128), BF16)],
        ),
    )
    return outs[0] if owners is None else outs


def weight_grad(sides, parts, cube, most, name):
    terms = len(sides[0])
    rows, width = sides[0][0].shape[0], sides[0][0].shape[1] // cube.size
    count = cube.size // 2
    sizes = [n[0][0].shape[-1] for _, n in parts]
    tile = functools.reduce(math.gcd, sizes, most)
    starts = [0]
    for size in sizes:
        starts.append(starts[-1] + size // tile)
    n_sides, n_parts, steps = len(sides), len(parts), starts[-1]
    half_steps = (steps + 1) // 2
    bounds = [0, half_steps, steps]
    place_a, place_b = ([0], [0])
    for m in reversed(cube.hops(0)):
        place_a = place_a + [k | m for k in place_a]
    for m in reversed(cube.hops(1)):
        place_b = place_b + [k | m for k in place_b]
    order_b = [place_a.index(k) for k in place_b]
    cut = count // 2

    def body(places_ref, *refs):
        d_refs = refs[: n_sides * terms * count]
        n_refs = refs[n_sides * terms * count :][: n_parts * terms]
        outs, turned = refs[-5:-1], refs[-1]
        j = pl.program_id(0)

        @pl.when(j == 0)
        def _():
            for k in range(n_sides * terms):
                for q in range(count):
                    turned[k, q * width : (q + 1) * width, :] = d_refs[k * count + q][...].T

        for p, (side, _) in enumerate(parts):
            for half in range(2):
                first, last = max(starts[p], bounds[half]), min(starts[p + 1], bounds[half + 1])
                if first >= last:
                    continue

                @pl.when((j >= first) & (j < last))
                def _(p=p, side=side, half=half):
                    acc = None
                    for t in range(terms):
                        term = mm(turned[side * terms + t], n_refs[p * terms + t][0])
                        acc = term if acc is None else acc + term
                    acc = acc.astype(BF16)
                    for to in range(count):
                        q = order_b[to] if half else to
                        out = outs[2 * half + to // cut]
                        at = to % cut
                        out[at * width : (at + 1) * width, :] = acc[q * width : (q + 1) * width, :]

    def n_spec(p, lead):
        last = starts[p + 1] - starts[p] - 1
        return pl.BlockSpec((1, rows, tile), lambda j, _: (lead, 0, jnp.clip(j - starts[p], 0, last)))

    in_specs = [
        pl.BlockSpec((rows, width), lambda j, p, q=q: (0, p[q])) for _ in range(n_sides * terms) for q in range(count)
    ]
    in_specs += [n_spec(p, lead) for p, (_, n) in enumerate(parts) for _, lead in n]
    operands = [cube.places(0)] + [d for side in sides for d in side for _ in range(count)]
    operands += [a for _, n in parts for a, _ in n]
    out_a = jax.ShapeDtypeStruct((cut * width, half_steps * tile), BF16)
    out_b = jax.ShapeDtypeStruct((cut * width, (steps - half_steps) * tile), BF16)
    spec_a = pl.BlockSpec((cut * width, tile), lambda j, _: (0, jnp.minimum(j, half_steps - 1)))
    spec_b = pl.BlockSpec((cut * width, tile), lambda j, _: (0, jnp.maximum(j - half_steps, 0)))
    keep_a, send_a, keep_b, send_b = kernel_call(
        body,
        name,
        2 * terms * rows * count * width * steps * tile,
        operands,
        [out_a, out_a, out_b, out_b],
        grid_spec=pltpu.PrefetchScalarGridSpec(
            num_scalar_prefetch=1,
            grid=(steps,),
            in_specs=in_specs,
            out_specs=[spec_a, spec_a, spec_b, spec_b],
            scratch_shapes=[pltpu.VMEM((n_sides * terms, count * width, rows), BF16)],
        ),
    )
    return (keep_a, send_a), (keep_b, send_b)


def attention_masked(queries, keys_all, segment, place):
    scale = 1.0 / math.sqrt(HEAD_DIM)
    allowed = (segment[:, None] == segment[None, :]) & (place[None, :] <= place[:, None])
    scores = jnp.einsum("qcgd,kcd->cgqk", queries, keys_all, preferred_element_type=F32) * scale
    return jnp.where(allowed, scores, -1e30)


def per_device(
    dp_size,
    tensor_size,
    tokens,
    seq_lengths,
    seq_group,
    attn_gain,
    w_query,
    w_key,
    w_value,
    w_out,
    mlp_gain,
    w_gate,
    w_up,
    w_down,
    cotangent,
):
    cube = Cube(dp_size)
    line = Line(tensor_size)
    scale = 1.0 / math.sqrt(HEAD_DIM)
    width_q, width_k = w_query.shape[1], w_key.shape[1]
    own_rows = tokens.shape[0]
    row_count = own_rows * tensor_size

    width_out, units = w_out.shape[0], w_gate.shape[1]

    rows_all = line.gather(tokens)
    gains = cube.gather_columns(jnp.stack([attn_gain, mlp_gain])).astype(F32)
    gain_one, gain_two = gains[:1], gains[1:]
    w_attn = lax.all_gather(jnp.concatenate([w_out.T, w_query, w_key, w_value], axis=1), "dp", axis=0, tiled=True)
    w_mlp = lax.all_gather(jnp.concatenate([w_gate, w_up, w_down.T], axis=1), "dp", axis=0, tiled=True)
    incoming_blocks = line.gather(after(cotangent, *rows_all))

    order = Order()
    attn_input, qkv = order(
        lambda *a: attention_in(a[:-2], a[-2], a[-1], width_out, line.owners), *rows_all, gain_one, w_attn
    )
    attn_input_other = cube.swap(attn_input, 1)
    tokens_f = tokens.astype(F32)
    normed_one, factor_one = norm_parts(tokens_f)
    heads_here = width_q // HEAD_DIM
    kv_here = width_k // HEAD_DIM
    head_group = heads_here // kv_here
    place = jnp.arange(row_count, dtype=jnp.int32)
    segment, position = layout(seq_lengths, seq_group, cube.me, place)
    cosine_table, sine_table = rope_tables(position, HEAD_DIM)
    queries = (
        rotate(qkv[:, :width_q].reshape(row_count, heads_here, HEAD_DIM), cosine_table, sine_table)
        .astype(BF16)
        .reshape(row_count, kv_here, head_group, HEAD_DIM)
    )
    keys_all = rotate(
        qkv[:, width_q : width_q + width_k].reshape(row_count, kv_here, HEAD_DIM), cosine_table, sine_table
    ).astype(BF16)
    values_all = qkv[:, width_q + width_k :].astype(BF16).reshape(row_count, kv_here, HEAD_DIM)
    scores = attention_masked(queries, keys_all, segment, place)
    row_max = jnp.max(scores, axis=-1, keepdims=True)
    exponent = jnp.exp(scores - row_max)
    row_sum = jnp.sum(exponent, axis=-1, keepdims=True)
    weights_low = (exponent / row_sum).astype(BF16)
    mixed = jnp.einsum("cgqk,kcd->qcgd", weights_low, values_all, preferred_element_type=F32)
    attended = mixed.reshape(row_count, heads_here * HEAD_DIM).astype(BF16)
    log_mass = row_max + jnp.log(row_sum)

    out_parts = order(
        lambda a, w: rows_product(a, [0], w, 0, "attention_out", line.owners),
        after(attended, *incoming_blocks[1:3])[None],
        w_attn,
    )
    attended_other = cube.swap(attended, 1)
    residual = order(lambda x, *terms: x + total32(terms), tokens_f, *line.scatter(out_parts))
    normed_two, factor_two = norm_parts(residual)
    mlp_blocks = line.gather((normed_two * gain_two).astype(BF16))

    mlp_input, incoming, unit_grads = order(
        lambda h, c, w: feed_forward(h, c, w, line.owners), mlp_blocks, incoming_blocks, w_mlp
    )
    mlp_others = [cube.swap(v, 1) for v in (mlp_input, incoming, unit_grads)]
    two_parts = order(lambda a, w: rows_product(a, [0, 1], w, 0, "feed_forward_rows_grad"), unit_grads, w_mlp)
    two_sum = lax.psum_scatter(two_parts, "tensor", scatter_dimension=0, tiled=True)

    def mlp_grad(h, c, n, h_other, c_other, n_other):
        parts = [(side, [(n, lead), (n_other, lead)]) for side, lead in ((0, 0), (0, 1), (1, 2))]
        return weight_grad([[h, h_other], [c, c_other]], parts, cube, 512, "feed_forward_grad")

    mlp_pairs = cube.first_hop(order(mlp_grad, mlp_input, incoming, unit_grads, *mlp_others))
    grad_residual = order(
        lambda c, g, n, f, t: c.astype(F32) + norm_back(t.astype(F32), g, n, f),
        cotangent,
        gain_two,
        normed_two,
        factor_two,
        two_sum,
    )
    grad_attn_rows = lax.all_gather(grad_residual.astype(BF16), "tensor", axis=0, tiled=True)
    block_parts = order(lambda a, w: rows_product(a, [2], w, 2 * units, "block_out"), unit_grads, w_mlp)
    block_parts, grad_attn_rows = lax.optimization_barrier((block_parts, grad_attn_rows))
    block_sum = lax.psum_scatter(block_parts, "tensor", scatter_dimension=0, tiled=True)
    rows_other = cube.swap(grad_attn_rows, 1)

    grad_attended = mm(grad_attn_rows, w_attn[:, :width_out]).astype(BF16)
    grad_block = grad_attended.reshape(row_count, kv_here, head_group, HEAD_DIM)
    scores = attention_masked(queries, keys_all, segment, place)
    probs = jnp.exp(scores - log_mass)
    weights_low = probs.astype(BF16)
    grad_probs = jnp.einsum("qcgd,kcd->cgqk", grad_block, values_all, preferred_element_type=F32)
    delta = jnp.sum(probs * grad_probs, axis=-1, keepdims=True)
    grad_scores = (probs * (grad_probs - delta)).astype(BF16)
    grad_queries = jnp.einsum("cgqk,kcd->qcgd", grad_scores, keys_all, preferred_element_type=F32) * scale
    grad_keys = jnp.einsum("cgqk,qcgd->kcd", grad_scores, queries, preferred_element_type=F32) * scale
    grad_values = jnp.einsum("cgqk,qcgd->kcd", weights_low, grad_block, preferred_element_type=F32)
    grad_queries = (
        rotate(grad_queries.reshape(row_count, heads_here, HEAD_DIM), cosine_table, -sine_table)
        .astype(BF16)
        .reshape(row_count, width_q)
    )
    grad_keys = rotate(grad_keys, cosine_table, -sine_table).astype(BF16).reshape(row_count, width_k)
    grad_qkv = jnp.concatenate(
        [grad_queries, grad_keys, grad_values.astype(BF16).reshape(row_count, width_k)], axis=1
    )
    one_parts = order(
        lambda a, w: rows_product(a, [0], w, width_out, "attention_rows_grad"), grad_qkv[None], w_attn
    )
    one_sum = lax.psum_scatter(after(one_parts, block_sum), "tensor", scatter_dimension=0, tiled=True)

    def attn_grad(y, y_other, h, h_other, a, a_other, g, g_other):
        parts = [(0, [(a[None], 0), (a_other[None], 0)]), (1, [(g[None], 0), (g_other[None], 0)])]
        return weight_grad([[y, y_other], [h, h_other]], parts, cube, 256, "attention_grad")

    attn_pairs = cube.first_hop(
        order(
            attn_grad,
            grad_attn_rows,
            rows_other,
            attn_input,
            attn_input_other,
            attended,
            attended_other,
            grad_qkv,
            cube.swap(grad_qkv, 1),
        )
    )
    block_out = order(lambda x, t: (x + t.astype(F32)).astype(BF16), residual, block_sum)
    mlp_terms = cube.other_hops(mlp_pairs, order)
    attn_terms = cube.other_hops(attn_pairs, order)

    def gain_terms(*pairs):
        return functools.reduce(lambda a, b: a + b, [jnp.sum(w.astype(F32) * g, axis=1) for w, g in pairs])

    def mlp_finals(terms, gate, up):
        sums = jnp.concatenate([total32(t) for t in terms], axis=1)
        gate_grad, up_grad, down_grad = sums[:, :units], sums[:, units : 2 * units], sums[:, 2 * units :].T
        return gain_terms((gate, gate_grad), (up, up_grad)), gate_grad, up_grad, down_grad

    mlp_gain_terms, gate_grad, up_grad, down_grad = order(mlp_finals, mlp_terms, w_gate, w_up)
    grad_tokens = order(
        lambda c, g, n, f, t: (c + norm_back(t.astype(F32), g, n, f)).astype(BF16),
        grad_residual,
        gain_one,
        normed_one,
        factor_one,
        one_sum,
    )
    attn_sum = jnp.concatenate([total32(t) for t in attn_terms], axis=1)
    out_grad, qkv_grad = attn_sum[:, :width_out].T, attn_sum[:, width_out:]
    query_grad = qkv_grad[:, :width_q]
    key_grad = qkv_grad[:, width_q : width_q + width_k]
    value_grad = qkv_grad[:, width_q + width_k :]
    attn_gain_terms = gain_terms((w_query, query_grad), (w_key, key_grad), (w_value, value_grad))
    gain_sums = line.total(jnp.stack([attn_gain_terms, mlp_gain_terms]))
    attn_gain_grad = gain_sums[0] / attn_gain.astype(F32)
    mlp_gain_grad = gain_sums[1] / mlp_gain.astype(F32)
    return (
        block_out,
        grad_tokens,
        attn_gain_grad,
        query_grad,
        key_grad,
        value_grad,
        out_grad,
        mlp_gain_grad,
        gate_grad,
        up_grad,
        down_grad,
    )


def solution(mesh):
    return jax.shard_map(
        functools.partial(per_device, mesh.shape["dp"], mesh.shape["tensor"]),
        mesh=mesh,
        in_specs=(
            P(("dp", "tensor"), None),
            P(),
            P(),
            P("dp"),
            P("dp", "tensor"),
            P("dp", "tensor"),
            P("dp", "tensor"),
            P("tensor", "dp"),
            P("dp"),
            P("dp", "tensor"),
            P("dp", "tensor"),
            P("tensor", "dp"),
            P(("dp", "tensor"), None),
        ),
        out_specs=(
            P(("dp", "tensor"), None),
            P(("dp", "tensor"), None),
            P("dp"),
            P("dp", "tensor"),
            P("dp", "tensor"),
            P("dp", "tensor"),
            P("tensor", "dp"),
            P("dp"),
            P("dp", "tensor"),
            P("dp", "tensor"),
            P("tensor", "dp"),
        ),
        check_vma=False,
    )
```

```python
import functools
import math

import jax
import jax.numpy as jnp
from jax import lax
from jax.experimental import pallas as pl
from jax.experimental.pallas import tpu as pltpu
from jax.sharding import PartitionSpec as P

HEAD_DIM = 64
EPSILON = 1e-05
ROPE_BASE = 500000.0
F32 = jnp.float32
BF16 = jnp.bfloat16


def rope_tables(position, width):
    half_width = width // 2
    steps_f = jnp.arange(half_width, dtype=F32)
    inverse = 1.0 / ROPE_BASE ** (steps_f * 2.0 / width)
    angles = position.astype(F32)[:, None] * inverse[None, :]
    cosine, sine = jnp.cos(angles), jnp.sin(angles)
    return jnp.concatenate([cosine] * 4 + [-sine, sine] * 2, axis=1)


def turned(values, cosine, sine):
    width = values.shape[1]
    half = HEAD_DIM // 2
    lane = lax.broadcasted_iota(jnp.int32, values.shape, 1)
    if width > HEAD_DIM:
        up, down = pltpu.roll(values, half, axis=1), pltpu.roll(values, width - half, axis=1)
        swapped = jnp.where(lane % HEAD_DIM < half, down, up)
    else:
        swapped = jnp.concatenate([values[:, half:], values[:, :half]], axis=1)
    return values * cosine[:, :width] + swapped * sine[:, :width]


def layout(seq_lengths, seq_group, group_id, row_count):
    owned = seq_group == group_id
    owned_len = jnp.where(owned, seq_lengths, 0)
    ends = jnp.where(owned, jnp.cumsum(owned_len), row_count + 1)
    row = jnp.arange(row_count, dtype=jnp.int32)
    offsets = jnp.sum((ends[None, :] <= row[:, None]).astype(jnp.int32) * owned_len[None, :], axis=1)
    return (ends.astype(jnp.int32), row - offsets)


def mm(left, right):
    return jnp.dot(left, right, preferred_element_type=F32)


def inner(left, right):
    return lax.dot_general(left, right, (((0,), (0,)), ((), ())), preferred_element_type=F32)


def outer(left, right):
    return lax.dot_general(left, right, (((1,), (1,)), ((), ())), preferred_element_type=F32)


def norm_parts(values):
    factor = lax.rsqrt(jnp.mean(values * values, axis=-1, keepdims=True) + EPSILON)
    return (values * factor, factor)


def norm_back(grad_rows, gain, normed, factor):
    scaled = grad_rows * gain
    return factor * (scaled - normed * jnp.mean(scaled * normed, axis=-1, keepdims=True))


def after(value, *deps):
    return lax.optimization_barrier((value,) + deps)[0]


class Line:
    def __init__(self, size):
        self.size = size
        self.index = lax.axis_index("tensor")
        self.owners = lax.rem(self.index - jnp.arange(size, dtype=jnp.int32) + size, size)

    def shift(self, v, r):
        return lax.ppermute(v, "tensor", [(i, (i + r) % self.size) for i in range(self.size)])

    def gather(self, v):
        return [v] + [self.shift(v, r) for r in range(1, self.size)]

    def scatter(self, parts):
        return [parts[0]] + [self.shift(parts[r], -r) for r in range(1, self.size)]

    def total(self, v):
        return functools.reduce(lambda a, b: a + b, [v] + [self.shift(v, r) for r in range(1, self.size)])


class Cube:
    def __init__(self, size):
        self.size = size
        self.me = lax.axis_index("dp")
        self.bits = [1 << b for b in range(size.bit_length() - 1)]

    def swap(self, v, m):
        return lax.ppermute(v, "dp", [(i, i ^ m) for i in range(self.size)])

    def gather_columns(self, v):
        for m in self.bits:
            other = self.swap(v, m)
            both = jnp.concatenate([v, other], axis=1), jnp.concatenate([other, v], axis=1)
            v = jnp.where((self.me & m) == 0, *both)
        return v

    def places(self, half):
        count = self.size // 2
        bits = self.hops(half)
        keys = [0]
        for m in reversed(bits):
            keys = keys + [k | m for k in keys]
        return self.me ^ jnp.array(keys[:count], jnp.int32)

    def hops(self, half):
        return self.bits[1:] if half else self.bits[:0:-1]

    def first_hop(self, pairs):
        return [(keep, self.swap(send, self.hops(half)[0])) for half, (keep, send) in enumerate(pairs)]

    def other_hops(self, pairs, order):
        terms = [list(pair) for pair in pairs]
        for hop in range(1, len(self.bits) - 1):
            rows = terms[0][-1].shape[0]
            sent = order(lambda *p: [total32([t[rows // 2 : rows] for t in ts]).astype(BF16) for ts in p], *terms)
            for half in range(2):
                terms[half].append(self.swap(sent[half], self.hops(half)[hop]))
        return terms


class Order:
    def __init__(self):
        self.last = None

    def __call__(self, step, *args):
        if self.last is not None:
            args, _ = lax.optimization_barrier((args, self.last))
        out = step(*args)
        self.last = jax.tree.leaves(out)[0]
        return out


def block_sum32(halves):
    return jnp.concatenate([total32([t[: terms[-1].shape[0]] for t in terms]) for terms in halves], axis=1)


def total32(terms):
    return functools.reduce(lambda a, b: a + b, [t.astype(F32) for t in terms])


def tile_of(size, most):
    while size % most:
        most //= 2
    return most


def kernel_call(body, name, flops, operands, out_shape, vmem=48, **kwargs):
    shapes = jax.tree.leaves(out_shape)
    moved = sum(math.prod(a.shape) * a.dtype.itemsize for a in list(operands) + shapes)
    return pl.pallas_call(
        body,
        out_shape=out_shape,
        name=name,
        cost_estimate=pl.CostEstimate(flops=flops, bytes_accessed=moved, transcendentals=0),
        compiler_params=pltpu.CompilerParams(vmem_limit_bytes=vmem << 20),
        **kwargs,
    )(*operands)


def whole(shape):
    return pl.BlockSpec(shape, lambda *_: (0,) * len(shape))


def attention_in(x_blocks, gain, w, skip, owners):
    count = len(x_blocks)
    rows, features = x_blocks[0].shape
    total, width = rows * count, w.shape[1] - skip
    tile = math.gcd(math.gcd(width, skip), 256)

    def body(owners_ref, *refs):
        x_refs, (gain_ref, w_ref, h_ref, out_ref) = refs[:count], refs[count:]

        @pl.when(pl.program_id(0) == 0)
        def _():
            for r in range(count):
                normed, _ = norm_parts(x_refs[r][...].astype(F32))
                at = pl.multiple_of(owners_ref[r] * rows, rows)
                h_ref[pl.ds(at, rows), :] = (normed * gain_ref[...]).astype(BF16)

        out_ref[...] = mm(h_ref[...], w_ref[...])

    return kernel_call(
        body,
        "attention_in",
        2 * total * features * width,
        (owners, *x_blocks, gain, w),
        (jax.ShapeDtypeStruct((total, features), BF16), jax.ShapeDtypeStruct((total, width), F32)),
        grid_spec=pltpu.PrefetchScalarGridSpec(
            num_scalar_prefetch=1,
            grid=(width // tile,),
            in_specs=[whole((rows, features))] * count
            + [whole((1, features)), pl.BlockSpec((features, tile), lambda j, _: (0, skip // tile + j))],
            out_specs=[whole((total, features)), pl.BlockSpec((total, tile), lambda j, _: (0, j))],
        ),
    )


def feed_forward(h_blocks, c_blocks, w, owners):
    count = len(h_blocks)
    rows, features = h_blocks[0].shape
    units = w.shape[1] // 3
    tile = tile_of(units, 256)
    steps = units // tile

    def body(owners_ref, *refs):
        h_refs, c_refs = refs[:count], refs[count : 2 * count]
        gate_ref, up_ref, down_ref, h_all, c_all, out_ref = refs[2 * count :]

        @pl.when(pl.program_id(0) == 0)
        def _():
            for r in range(count):
                at = pl.multiple_of(owners_ref[r] * rows, rows)
                h_all[pl.ds(at, rows), :] = h_refs[r][...]
                c_all[pl.ds(at, rows), :] = c_refs[r][...]

        gate = mm(h_all[...], gate_ref[...])
        up = mm(h_all[...], up_ref[...])
        grad_hidden = mm(c_all[...], down_ref[...])
        sig = 1.0 / (1.0 + jnp.exp(-gate))
        silu = gate * sig
        out_ref[0] = (grad_hidden * up * (sig * (1.0 + gate * (1.0 - sig)))).astype(BF16)
        out_ref[1] = (grad_hidden * silu).astype(BF16)
        out_ref[2] = (silu * up).astype(BF16)

    total = rows * count
    wide = jax.ShapeDtypeStruct((total, features), BF16)
    return kernel_call(
        body,
        "feed_forward",
        6 * total * features * units,
        (owners, *h_blocks, *c_blocks, w, w, w),
        (wide, wide, jax.ShapeDtypeStruct((3, total, units), BF16)),
        grid_spec=pltpu.PrefetchScalarGridSpec(
            num_scalar_prefetch=1,
            grid=(steps,),
            in_specs=[whole((rows, features))] * (2 * count)
            + [pl.BlockSpec((features, tile), lambda j, _, k=k: (0, k * steps + j)) for k in range(3)],
            out_specs=[whole((total, features))] * 2 + [pl.BlockSpec((3, total, tile), lambda j, _: (0, 0, j))],
        ),
    )


def rows_product(a, leads, w, first, name, owners=None):
    rows, units = a.shape[1:]
    features = w.shape[0]
    tile = tile_of(features, 512 if units * len(leads) > 1024 else 1024)
    count = 1 if owners is None else owners.shape[0]
    block = rows // count
    width = units * len(leads)
    aligned = first % width == 0

    def body(owners_ref, *refs):
        a_refs, w_ref, outs, turned = refs[: len(leads)], refs[len(leads)], refs[len(leads) + 1 : -1], refs[-1]
        if owners is not None:

            @pl.when(pl.program_id(0) == 0)
            def _():
                for r in range(count):
                    at = pl.multiple_of(owners_ref[r] * block, block)
                    for k in range(len(leads)):
                        turned[k, r * block : (r + 1) * block, :] = a_refs[k][0, pl.ds(at, block), :]

        at = 0 if aligned else first
        acc = None
        for k, a_ref in enumerate(a_refs):
            term = outer(a_ref[0] if owners is None else turned[k], w_ref[:, at : at + units])
            acc = term if acc is None else acc + term
            at += units
        for r in range(count):
            outs[r][...] = acc[r * block : (r + 1) * block, :].astype(BF16)

    spec = pl.BlockSpec((tile, width), lambda j, _: (j, first // width))
    if not aligned:
        spec = pl.BlockSpec((tile, w.shape[1]), lambda j, _: (j, 0))
    outs = kernel_call(
        body,
        name,
        2 * rows * features * width,
        [jnp.zeros((1,), jnp.int32) if owners is None else owners] + [a] * len(leads) + [w],
        [jax.ShapeDtypeStruct((block, features), BF16)] * count,
        grid_spec=pltpu.PrefetchScalarGridSpec(
            num_scalar_prefetch=1,
            grid=(features // tile,),
            in_specs=[pl.BlockSpec((1, rows, units), lambda j, _, k=k: (k, 0, 0)) for k in leads] + [spec],
            out_specs=[pl.BlockSpec((block, tile), lambda j, _: (0, j))] * count,
            scratch_shapes=[pltpu.VMEM((len(leads), rows, units) if owners is not None else (1, 16, 128), BF16)],
        ),
    )
    return outs[0] if owners is None else outs


def weight_grad(sides, parts, cube, most, name):
    terms = len(sides[0])
    rows, width = sides[0][0].shape[0], sides[0][0].shape[1] // cube.size
    count = cube.size // 2
    sizes = [n[0][0].shape[-1] for _, n in parts]
    tile = functools.reduce(math.gcd, sizes, most)
    starts = [0]
    for size in sizes:
        starts.append(starts[-1] + size // tile)
    n_sides, n_parts, steps = len(sides), len(parts), starts[-1]
    half_steps = (steps + 1) // 2
    bounds = [0, half_steps, steps]
    place_a, place_b = ([0], [0])
    for m in reversed(cube.hops(0)):
        place_a = place_a + [k | m for k in place_a]
    for m in reversed(cube.hops(1)):
        place_b = place_b + [k | m for k in place_b]
    order_b = [place_a.index(k) for k in place_b]
    cut = count // 2

    def body(places_ref, *refs):
        d_refs = refs[: n_sides * terms * count]
        n_refs = refs[n_sides * terms * count :][: n_parts * terms]
        outs, turned = refs[-5:-1], refs[-1]
        j = pl.program_id(0)

        @pl.when(j == 0)
        def _():
            for k in range(n_sides * terms):
                for q in range(count):
                    turned[k, q * width : (q + 1) * width, :] = d_refs[k * count + q][...].T

        for p, (side, _) in enumerate(parts):
            for half in range(2):
                first, last = max(starts[p], bounds[half]), min(starts[p + 1], bounds[half + 1])
                if first >= last:
                    continue

                @pl.when((j >= first) & (j < last))
                def _(p=p, side=side, half=half):
                    acc = None
                    for t in range(terms):
                        term = mm(turned[side * terms + t], n_refs[p * terms + t][0])
                        acc = term if acc is None else acc + term
                    acc = acc.astype(BF16)
                    for to in range(count):
                        q = order_b[to] if half else to
                        out = outs[2 * half + to // cut]
                        at = to % cut
                        out[at * width : (at + 1) * width, :] = acc[q * width : (q + 1) * width, :]

    def n_spec(p, lead):
        last = starts[p + 1] - starts[p] - 1
        return pl.BlockSpec((1, rows, tile), lambda j, _: (lead, 0, jnp.clip(j - starts[p], 0, last)))

    in_specs = [
        pl.BlockSpec((rows, width), lambda j, p, q=q: (0, p[q])) for _ in range(n_sides * terms) for q in range(count)
    ]
    in_specs += [n_spec(p, lead) for p, (_, n) in enumerate(parts) for _, lead in n]
    operands = [cube.places(0)] + [d for side in sides for d in side for _ in range(count)]
    operands += [a for _, n in parts for a, _ in n]
    out_a = jax.ShapeDtypeStruct((cut * width, half_steps * tile), BF16)
    out_b = jax.ShapeDtypeStruct((cut * width, (steps - half_steps) * tile), BF16)
    spec_a = pl.BlockSpec((cut * width, tile), lambda j, _: (0, jnp.minimum(j, half_steps - 1)))
    spec_b = pl.BlockSpec((cut * width, tile), lambda j, _: (0, jnp.maximum(j - half_steps, 0)))
    keep_a, send_a, keep_b, send_b = kernel_call(
        body,
        name,
        2 * terms * rows * count * width * steps * tile,
        operands,
        [out_a, out_a, out_b, out_b],
        grid_spec=pltpu.PrefetchScalarGridSpec(
            num_scalar_prefetch=1,
            grid=(steps,),
            in_specs=in_specs,
            out_specs=[spec_a, spec_a, spec_b, spec_b],
            scratch_shapes=[pltpu.VMEM((n_sides * terms, count * width, rows), BF16)],
        ),
    )
    return (keep_a, send_a), (keep_b, send_b)


def head_columns(heads, kv):
    keys, values = heads * HEAD_DIM, (heads + kv) * HEAD_DIM
    for h in range(heads):
        c = h // (heads // kv)
        yield (
            slice(h * HEAD_DIM, (h + 1) * HEAD_DIM),
            slice(keys + c * HEAD_DIM, keys + (c + 1) * HEAD_DIM),
            slice(values + c * HEAD_DIM, values + (c + 1) * HEAD_DIM),
        )


def segments(ends_ref, count, place):
    found = jnp.zeros_like(place)
    for i in range(count):
        found += (ends_ref[i] <= place).astype(jnp.int32)
    return found


def allowed_pairs(ends_ref, count, j, block, rows):
    query = j * block + lax.broadcasted_iota(jnp.int32, (block, 128), 0)
    key = lax.broadcasted_iota(jnp.int32, (8, rows), 1)
    query_segment, key_segment = segments(ends_ref, count, query)[:, :1], segments(ends_ref, count, key)[:1]
    return (query_segment == key_segment) & (key[:1] <= query[:, :1])


def turn_heads(read, write, columns, cosine, sine):
    step = 2 * HEAD_DIM
    for at in range(0, columns, step):
        cut = slice(at, min(at + step, columns))
        write(cut, turned(read(cut), cosine, sine).astype(BF16))


def attention_forward(ends, qkv, table, heads, kv):
    rows, width = qkv.shape
    block = tile_of(rows, 256)
    turn_width = (heads + kv) * HEAD_DIM
    at_sine = table.shape[1] // 2
    scale = 1.0 / math.sqrt(HEAD_DIM)

    def body(ends_ref, qkv_ref, table_ref, low_ref, out_ref, mass_ref):
        j = pl.program_id(0)

        @pl.when(j == 0)
        def _():
            def write(cut, v):
                low_ref[:, cut] = v

            turn_heads(lambda cut: qkv_ref[:, cut], write, turn_width, table_ref[:, :at_sine], table_ref[:, at_sine:])
            low_ref[:, turn_width:] = qkv_ref[:, turn_width:].astype(BF16)

        allowed = allowed_pairs(ends_ref, ends.shape[0], j, block, rows)
        here = pl.ds(pl.multiple_of(j * block, block), block)
        lane = lax.broadcasted_iota(jnp.int32, (block, 128), 1)
        mass = jnp.zeros((block, 128), F32)
        for h, (q_at, k_at, v_at) in enumerate(head_columns(heads, kv)):
            scores = outer(low_ref[here, q_at], low_ref[:, k_at]) * scale
            scores = jnp.where(allowed, scores, -1e30)
            row_max = jnp.max(scores, axis=1, keepdims=True)
            weights = jnp.exp(scores - row_max)
            row_sum = jnp.sum(weights, axis=1, keepdims=True)
            weights_low = (weights / row_sum).astype(BF16)
            out_ref[:, q_at] = mm(weights_low, low_ref[:, v_at]).astype(BF16)
            mass = jnp.where(lane == h, row_max + jnp.log(row_sum), mass)
        mass_ref[...] = mass

    return kernel_call(
        body,
        "attention_forward",
        4 * rows * rows * heads * HEAD_DIM,
        (ends, qkv, table),
        (
            jax.ShapeDtypeStruct((rows, width), BF16),
            jax.ShapeDtypeStruct((rows, heads * HEAD_DIM), BF16),
            jax.ShapeDtypeStruct((rows, 128), F32),
        ),
        grid_spec=pltpu.PrefetchScalarGridSpec(
            num_scalar_prefetch=1,
            grid=(rows // block,),
            in_specs=[whole((rows, width)), whole(table.shape)],
            out_specs=[
                whole((rows, width)),
                pl.BlockSpec((block, heads * HEAD_DIM), lambda j, _: (j, 0)),
                pl.BlockSpec((block, 128), lambda j, _: (j, 0)),
            ],
        ),
    )


def attention_backward(ends, grad_rows, w, low, mass, table, heads, kv):
    rows, features = grad_rows.shape
    width, out_width = low.shape[1], heads * HEAD_DIM
    block = tile_of(rows, 256)
    scale = 1.0 / math.sqrt(HEAD_DIM)

    at_sine = table.shape[1] // 2

    def body(ends_ref, grad_ref, w_ref, low_ref, mass_ref, table_ref, out_ref, low_grad, q_grad, k_grad, v_grad):
        j = pl.program_id(0)

        @pl.when(j == 0)
        def _():
            low_grad[...] = mm(grad_ref[...], w_ref[...]).astype(BF16)
            k_grad[...] = jnp.zeros_like(k_grad)
            v_grad[...] = jnp.zeros_like(v_grad)

        allowed = allowed_pairs(ends_ref, ends.shape[0], j, block, rows)
        here = pl.ds(pl.multiple_of(j * block, block), block)
        for h, (q_at, k_at, v_at) in enumerate(head_columns(heads, kv)):
            query, grad = low_ref[here, q_at], low_grad[here, q_at]
            scores = outer(query, low_ref[:, k_at]) * scale
            probs = jnp.exp(jnp.where(allowed, scores, -1e30) - mass_ref[:, h : h + 1])
            grad_probs = outer(grad, low_ref[:, v_at])
            delta = jnp.sum(probs * grad_probs, axis=1, keepdims=True)
            grad_scores = (probs * (grad_probs - delta)).astype(BF16)
            q_grad[:, q_at] = mm(grad_scores, low_ref[:, k_at]) * scale
            c = h // (heads // kv)
            kv_at = slice(c * HEAD_DIM, (c + 1) * HEAD_DIM)
            k_grad[:, kv_at] += inner(grad_scores, query)
            v_grad[:, kv_at] += inner(probs.astype(BF16), grad)

        def write_q(cut, v):
            out_ref[here, cut] = v

        def write_k(cut, v):
            out_ref[:, out_width + cut.start : out_width + cut.stop] = v

        turn_heads(lambda cut: q_grad[:, cut], write_q, out_width, table_ref[here, :at_sine], -table_ref[here, at_sine:])

        @pl.when(j == pl.num_programs(0) - 1)
        def _():
            turn_heads(lambda cut: k_grad[:, cut] * scale, write_k, kv * HEAD_DIM, table_ref[:, :at_sine], -table_ref[:, at_sine:])
            out_ref[:, out_width + kv * HEAD_DIM :] = v_grad[...].astype(BF16)

    return kernel_call(
        body,
        "attention_backward",
        10 * rows * rows * heads * HEAD_DIM + 2 * rows * features * out_width,
        (ends, grad_rows, w, low, mass, table),
        jax.ShapeDtypeStruct((rows, width), BF16),
        grid_spec=pltpu.PrefetchScalarGridSpec(
            num_scalar_prefetch=1,
            grid=(rows // block,),
            in_specs=[
                whole((rows, features)),
                pl.BlockSpec((features, out_width), lambda j, _: (0, 0)),
                whole((rows, width)),
                pl.BlockSpec((block, 128), lambda j, _: (j, 0)),
                whole(table.shape),
            ],
            out_specs=whole((rows, width)),
            scratch_shapes=[
                pltpu.VMEM((rows, out_width), BF16),
                pltpu.VMEM((block, out_width), F32),
                pltpu.VMEM((rows, kv * HEAD_DIM), F32),
                pltpu.VMEM((rows, kv * HEAD_DIM), F32),
            ],
        ),
    )


def per_device(
    dp_size,
    tensor_size,
    tokens,
    seq_lengths,
    seq_group,
    attn_gain,
    w_query,
    w_key,
    w_value,
    w_out,
    mlp_gain,
    w_gate,
    w_up,
    w_down,
    cotangent,
):
    cube = Cube(dp_size)
    line = Line(tensor_size)
    width_q, width_k = w_query.shape[1], w_key.shape[1]
    own_rows = tokens.shape[0]
    row_count = own_rows * tensor_size

    width_out, units = w_out.shape[0], w_gate.shape[1]

    rows_all = line.gather(tokens)
    gains = cube.gather_columns(jnp.stack([attn_gain, mlp_gain])).astype(F32)
    gain_one, gain_two = gains[:1], gains[1:]
    w_attn = lax.all_gather(jnp.concatenate([w_out.T, w_query, w_key, w_value], axis=1), "dp", axis=0, tiled=True)
    w_mlp = lax.all_gather(jnp.concatenate([w_gate, w_up, w_down.T], axis=1), "dp", axis=0, tiled=True)
    incoming_blocks = line.gather(after(cotangent, *rows_all))

    order = Order()
    attn_input, qkv = order(
        lambda *a: attention_in(a[:-2], a[-2], a[-1], width_out, line.owners), *rows_all, gain_one, w_attn
    )
    attn_input_other = cube.swap(attn_input, 1)
    tokens_f = tokens.astype(F32)
    normed_one, factor_one = norm_parts(tokens_f)
    heads_here = width_q // HEAD_DIM
    kv_here = width_k // HEAD_DIM
    ends, position = layout(seq_lengths, seq_group, cube.me, row_count)
    table = rope_tables(position, HEAD_DIM)
    low_qkv, attended, log_mass = order(lambda *a: attention_forward(*a, heads_here, kv_here), ends, qkv, table)

    out_parts = order(
        lambda a, w: rows_product(a, [0], w, 0, "attention_out", line.owners),
        after(attended, incoming_blocks[1])[None],
        w_attn,
    )
    attended_other = cube.swap(attended, 1)
    residual = order(lambda x, *terms: x + total32(terms), tokens_f, *line.scatter(out_parts))
    normed_two, factor_two = norm_parts(residual)
    mlp_blocks = line.gather((normed_two * gain_two).astype(BF16))

    mlp_input, incoming, unit_grads = order(
        lambda h, c, w: feed_forward(h, c, w, line.owners),
        mlp_blocks,
        incoming_blocks,
        after(w_mlp, attn_input_other, attended_other),
    )
    mlp_others = [cube.swap(v, 1) for v in (mlp_input, incoming, unit_grads)]
    two_parts = order(lambda a, w: rows_product(a, [0, 1], w, 0, "feed_forward_rows_grad"), unit_grads, w_mlp)
    two_sum = lax.psum_scatter(two_parts, "tensor", scatter_dimension=0, tiled=True)

    def mlp_grad(h, c, n, h_other, c_other, n_other):
        parts = [(side, [(n, lead), (n_other, lead)]) for side, lead in ((0, 0), (0, 1), (1, 2))]
        return weight_grad([[h, h_other], [c, c_other]], parts, cube, 512, "feed_forward_grad")

    mlp_pairs = cube.first_hop(order(mlp_grad, mlp_input, incoming, unit_grads, *mlp_others))
    grad_residual = order(
        lambda c, g, n, f, t: c.astype(F32) + norm_back(t.astype(F32), g, n, f),
        cotangent,
        gain_two,
        normed_two,
        factor_two,
        two_sum,
    )
    grad_attn_rows = lax.all_gather(grad_residual.astype(BF16), "tensor", axis=0, tiled=True)
    block_parts = order(lambda a, w: rows_product(a, [2], w, 2 * units, "block_out"), unit_grads, w_mlp)
    block_parts, grad_attn_rows = lax.optimization_barrier((block_parts, grad_attn_rows))
    block_sum = lax.psum_scatter(block_parts, "tensor", scatter_dimension=0, tiled=True)
    rows_other = cube.swap(grad_attn_rows, 1)

    grad_qkv = order(
        lambda *a: attention_backward(*a, heads_here, kv_here), ends, grad_attn_rows, w_attn, low_qkv, log_mass, table
    )
    mlp_terms = cube.other_hops(mlp_pairs, order)
    one_parts = order(
        lambda a, w: rows_product(a, [0], w, width_out, "attention_rows_grad"), grad_qkv[None], w_attn
    )
    one_sum = lax.psum_scatter(after(one_parts, block_sum), "tensor", scatter_dimension=0, tiled=True)


    def attn_grad(y, y_other, h, h_other, a, a_other, g, g_other):
        parts = [(0, [(a[None], 0), (a_other[None], 0)]), (1, [(g[None], 0), (g_other[None], 0)])]
        return weight_grad([[y, y_other], [h, h_other]], parts, cube, 256, "attention_grad")

    attn_pairs = cube.first_hop(
        order(
            attn_grad,
            grad_attn_rows,
            rows_other,
            attn_input,
            attn_input_other,
            attended,
            attended_other,
            grad_qkv,
            cube.swap(grad_qkv, 1),
        )
    )
    block_out = order(lambda x, t: (x + t.astype(F32)).astype(BF16), residual, block_sum)
    attn_terms = cube.other_hops(attn_pairs, order)

    def gain_terms(*pairs):
        return functools.reduce(lambda a, b: a + b, [jnp.sum(w.astype(F32) * g, axis=1) for w, g in pairs])

    def mlp_finals(terms, gate, up):
        sums = block_sum32(terms)
        gate_grad, up_grad, down_grad = sums[:, :units], sums[:, units : 2 * units], sums[:, 2 * units :].T
        return gain_terms((gate, gate_grad), (up, up_grad)), gate_grad, up_grad, down_grad

    mlp_gain_terms, gate_grad, up_grad, down_grad = order(mlp_finals, mlp_terms, w_gate, w_up)
    grad_tokens = order(
        lambda c, g, n, f, t: (c + norm_back(t.astype(F32), g, n, f)).astype(BF16),
        grad_residual,
        gain_one,
        normed_one,
        factor_one,
        one_sum,
    )
    attn_sum = block_sum32(attn_terms)
    out_grad, qkv_grad = attn_sum[:, :width_out].T, attn_sum[:, width_out:]
    query_grad = qkv_grad[:, :width_q]
    key_grad = qkv_grad[:, width_q : width_q + width_k]
    value_grad = qkv_grad[:, width_q + width_k :]
    attn_gain_terms = gain_terms((w_query, query_grad), (w_key, key_grad), (w_value, value_grad))
    gain_sums = line.total(jnp.stack([attn_gain_terms, mlp_gain_terms]))
    attn_gain_grad = gain_sums[0] / attn_gain.astype(F32)
    mlp_gain_grad = gain_sums[1] / mlp_gain.astype(F32)
    return (
        block_out,
        grad_tokens,
        attn_gain_grad,
        query_grad,
        key_grad,
        value_grad,
        out_grad,
        mlp_gain_grad,
        gate_grad,
        up_grad,
        down_grad,
    )


def solution(mesh):
    return jax.shard_map(
        functools.partial(per_device, mesh.shape["dp"], mesh.shape["tensor"]),
        mesh=mesh,
        in_specs=(
            P(("dp", "tensor"), None),
            P(),
            P(),
            P("dp"),
            P("dp", "tensor"),
            P("dp", "tensor"),
            P("dp", "tensor"),
            P("tensor", "dp"),
            P("dp"),
            P("dp", "tensor"),
            P("dp", "tensor"),
            P("tensor", "dp"),
            P(("dp", "tensor"), None),
        ),
        out_specs=(
            P(("dp", "tensor"), None),
            P(("dp", "tensor"), None),
            P("dp"),
            P("dp", "tensor"),
            P("dp", "tensor"),
            P("dp", "tensor"),
            P("tensor", "dp"),
            P("dp"),
            P("dp", "tensor"),
            P("dp", "tensor"),
            P("tensor", "dp"),
        ),
        check_vma=False,
    )
```

```python
import functools
import math

import jax
import jax.numpy as jnp
from jax import lax
from jax.experimental import pallas as pl
from jax.experimental.pallas import tpu as pltpu
from jax.sharding import PartitionSpec as P

HEAD_DIM = 64
EPSILON = 1e-05
ROPE_BASE = 500000.0
F32 = jnp.float32
BF16 = jnp.bfloat16


def rope_tables(position, width):
    half_width = width // 2
    steps_f = jnp.arange(half_width, dtype=F32)
    inverse = 1.0 / ROPE_BASE ** (steps_f * 2.0 / width)
    angles = position.astype(F32)[:, None] * inverse[None, :]
    cosine, sine = jnp.cos(angles), jnp.sin(angles)
    return jnp.concatenate([cosine] * 4 + [-sine, sine] * 2, axis=1)


def turned(values, cosine, sine):
    width = values.shape[1]
    half = HEAD_DIM // 2
    lane = lax.broadcasted_iota(jnp.int32, values.shape, 1)
    if width > HEAD_DIM:
        up, down = pltpu.roll(values, half, axis=1), pltpu.roll(values, width - half, axis=1)
        swapped = jnp.where(lane % HEAD_DIM < half, down, up)
    else:
        swapped = jnp.concatenate([values[:, half:], values[:, :half]], axis=1)
    return values * cosine[:, :width] + swapped * sine[:, :width]


def layout(seq_lengths, seq_group, group_id, row_count):
    owned = seq_group == group_id
    owned_len = jnp.where(owned, seq_lengths, 0)
    ends = jnp.where(owned, jnp.cumsum(owned_len), row_count + 1)
    row = jnp.arange(row_count, dtype=jnp.int32)
    offsets = jnp.sum((ends[None, :] <= row[:, None]).astype(jnp.int32) * owned_len[None, :], axis=1)
    return (ends.astype(jnp.int32), row - offsets)


def mm(left, right):
    return jnp.dot(left, right, preferred_element_type=F32)


def inner(left, right):
    return lax.dot_general(left, right, (((0,), (0,)), ((), ())), preferred_element_type=F32)


def outer(left, right):
    return lax.dot_general(left, right, (((1,), (1,)), ((), ())), preferred_element_type=F32)


def norm_parts(values):
    factor = lax.rsqrt(jnp.mean(values * values, axis=-1, keepdims=True) + EPSILON)
    return (values * factor, factor)


def norm_back(grad_rows, gain, normed, factor):
    scaled = grad_rows * gain
    return factor * (scaled - normed * jnp.mean(scaled * normed, axis=-1, keepdims=True))


def after(value, *deps):
    return lax.optimization_barrier((value,) + deps)[0]


class Line:
    def __init__(self, size):
        self.size = size
        self.index = lax.axis_index("tensor")
        self.owners = lax.rem(self.index - jnp.arange(size, dtype=jnp.int32) + size, size)

    def shift(self, v, r):
        return lax.ppermute(v, "tensor", [(i, (i + r) % self.size) for i in range(self.size)])

    def gather(self, v):
        return [v] + [self.shift(v, r) for r in range(1, self.size)]

    def scatter(self, parts):
        return [parts[0]] + [self.shift(parts[r], -r) for r in range(1, self.size)]

    def total(self, v):
        return functools.reduce(lambda a, b: a + b, [v] + [self.shift(v, r) for r in range(1, self.size)])


class Cube:
    def __init__(self, size):
        self.size = size
        self.me = lax.axis_index("dp")
        self.bits = [1 << b for b in range(size.bit_length() - 1)]

    def swap(self, v, m):
        return lax.ppermute(v, "dp", [(i, i ^ m) for i in range(self.size)])

    def gather_columns(self, v):
        for m in self.bits:
            other = self.swap(v, m)
            both = jnp.concatenate([v, other], axis=1), jnp.concatenate([other, v], axis=1)
            v = jnp.where((self.me & m) == 0, *both)
        return v

    def places(self, half):
        count = self.size // 2
        bits = self.hops(half)
        keys = [0]
        for m in reversed(bits):
            keys = keys + [k | m for k in keys]
        return self.me ^ jnp.array(keys[:count], jnp.int32)

    def hops(self, half):
        return self.bits[1:] if half else self.bits[:0:-1]

    def first_hop(self, pairs):
        return [(keep, self.swap(send, self.hops(half)[0])) for half, (keep, send) in enumerate(pairs)]

    def other_hops(self, pairs, order):
        terms = [list(pair) for pair in pairs]
        for hop in range(1, len(self.bits) - 1):
            rows = terms[0][-1].shape[0]
            sent = order(lambda *p: [total32([t[rows // 2 : rows] for t in ts]).astype(BF16) for ts in p], *terms)
            for half in range(2):
                terms[half].append(self.swap(sent[half], self.hops(half)[hop]))
        return terms


class Order:
    def __init__(self):
        self.last = None

    def __call__(self, step, *args):
        if self.last is not None:
            args, _ = lax.optimization_barrier((args, self.last))
        out = step(*args)
        self.last = jax.tree.leaves(out)[0]
        return out


def block_sum32(halves):
    return jnp.concatenate([total32([t[: terms[-1].shape[0]] for t in terms]) for terms in halves], axis=1)


def total32(terms):
    return functools.reduce(lambda a, b: a + b, [t.astype(F32) for t in terms])


def tile_of(size, most):
    while size % most:
        most //= 2
    return most


def kernel_call(body, name, flops, operands, out_shape, vmem=48, **kwargs):
    shapes = jax.tree.leaves(out_shape)
    moved = sum(math.prod(a.shape) * a.dtype.itemsize for a in list(operands) + shapes)
    return pl.pallas_call(
        body,
        out_shape=out_shape,
        name=name,
        cost_estimate=pl.CostEstimate(flops=flops, bytes_accessed=moved, transcendentals=0),
        compiler_params=pltpu.CompilerParams(vmem_limit_bytes=vmem << 20),
        **kwargs,
    )(*operands)


def whole(shape):
    return pl.BlockSpec(shape, lambda *_: (0,) * len(shape))


def feed_forward(h_blocks, c_blocks, w, owners):
    count = len(h_blocks)
    rows, features = h_blocks[0].shape
    units = w.shape[1] // 3
    tile = tile_of(units, 256)
    steps = units // tile

    def body(owners_ref, *refs):
        h_refs, c_refs = refs[:count], refs[count : 2 * count]
        gate_ref, up_ref, down_ref, h_all, c_all, out_ref = refs[2 * count :]

        @pl.when(pl.program_id(0) == 0)
        def _():
            for r in range(count):
                at = pl.multiple_of(owners_ref[r] * rows, rows)
                h_all[pl.ds(at, rows), :] = h_refs[r][...]
                c_all[pl.ds(at, rows), :] = c_refs[r][...]

        gate = mm(h_all[...], gate_ref[...])
        up = mm(h_all[...], up_ref[...])
        grad_hidden = mm(c_all[...], down_ref[...])
        sig = 1.0 / (1.0 + jnp.exp(-gate))
        silu = gate * sig
        out_ref[0] = (grad_hidden * up * (sig * (1.0 + gate * (1.0 - sig)))).astype(BF16)
        out_ref[1] = (grad_hidden * silu).astype(BF16)
        out_ref[2] = (silu * up).astype(BF16)

    total = rows * count
    wide = jax.ShapeDtypeStruct((total, features), BF16)
    return kernel_call(
        body,
        "feed_forward",
        6 * total * features * units,
        (owners, *h_blocks, *c_blocks, w, w, w),
        (wide, wide, jax.ShapeDtypeStruct((3, total, units), BF16)),
        grid_spec=pltpu.PrefetchScalarGridSpec(
            num_scalar_prefetch=1,
            grid=(steps,),
            in_specs=[whole((rows, features))] * (2 * count)
            + [pl.BlockSpec((features, tile), lambda j, _, k=k: (0, k * steps + j)) for k in range(3)],
            out_specs=[whole((total, features))] * 2 + [pl.BlockSpec((3, total, tile), lambda j, _: (0, 0, j))],
        ),
    )


def rows_product(a, leads, w, first, name, owners=None):
    rows, units = a.shape[1:]
    features = w.shape[0]
    tile = tile_of(features, 512 if units * len(leads) > 1024 else 1024)
    count = 1 if owners is None else owners.shape[0]
    block = rows // count
    width = units * len(leads)
    aligned = first % width == 0

    def body(owners_ref, *refs):
        a_refs, w_ref, outs, turned = refs[: len(leads)], refs[len(leads)], refs[len(leads) + 1 : -1], refs[-1]
        if owners is not None:

            @pl.when(pl.program_id(0) == 0)
            def _():
                for r in range(count):
                    at = pl.multiple_of(owners_ref[r] * block, block)
                    for k in range(len(leads)):
                        turned[k, r * block : (r + 1) * block, :] = a_refs[k][0, pl.ds(at, block), :]

        at = 0 if aligned else first
        acc = None
        for k, a_ref in enumerate(a_refs):
            term = outer(a_ref[0] if owners is None else turned[k], w_ref[:, at : at + units])
            acc = term if acc is None else acc + term
            at += units
        for r in range(count):
            outs[r][...] = acc[r * block : (r + 1) * block, :].astype(BF16)

    spec = pl.BlockSpec((tile, width), lambda j, _: (j, first // width))
    if not aligned:
        spec = pl.BlockSpec((tile, w.shape[1]), lambda j, _: (j, 0))
    outs = kernel_call(
        body,
        name,
        2 * rows * features * width,
        [jnp.zeros((1,), jnp.int32) if owners is None else owners] + [a] * len(leads) + [w],
        [jax.ShapeDtypeStruct((block, features), BF16)] * count,
        grid_spec=pltpu.PrefetchScalarGridSpec(
            num_scalar_prefetch=1,
            grid=(features // tile,),
            in_specs=[pl.BlockSpec((1, rows, units), lambda j, _, k=k: (k, 0, 0)) for k in leads] + [spec],
            out_specs=[pl.BlockSpec((block, tile), lambda j, _: (0, j))] * count,
            scratch_shapes=[pltpu.VMEM((len(leads), rows, units) if owners is not None else (1, 16, 128), BF16)],
        ),
    )
    return outs[0] if owners is None else outs


def weight_grad(sides, parts, cube, most, name):
    terms = len(sides[0])
    rows, width = sides[0][0].shape[0], sides[0][0].shape[1] // cube.size
    count = cube.size // 2
    sizes = [n[0][0].shape[-1] for _, n in parts]
    tile = functools.reduce(math.gcd, sizes, most)
    starts = [0]
    for size in sizes:
        starts.append(starts[-1] + size // tile)
    n_sides, n_parts, steps = len(sides), len(parts), starts[-1]
    half_steps = (steps + 1) // 2
    bounds = [0, half_steps, steps]
    place_a, place_b = ([0], [0])
    for m in reversed(cube.hops(0)):
        place_a = place_a + [k | m for k in place_a]
    for m in reversed(cube.hops(1)):
        place_b = place_b + [k | m for k in place_b]
    order_b = [place_a.index(k) for k in place_b]
    cut = count // 2

    def body(places_ref, *refs):
        d_refs = refs[: n_sides * terms * count]
        n_refs = refs[n_sides * terms * count :][: n_parts * terms]
        outs, turned = refs[-5:-1], refs[-1]
        j = pl.program_id(0)

        @pl.when(j == 0)
        def _():
            for k in range(n_sides * terms):
                for q in range(count):
                    turned[k, q * width : (q + 1) * width, :] = d_refs[k * count + q][...].T

        for p, (side, _) in enumerate(parts):
            for half in range(2):
                first, last = max(starts[p], bounds[half]), min(starts[p + 1], bounds[half + 1])
                if first >= last:
                    continue

                @pl.when((j >= first) & (j < last))
                def _(p=p, side=side, half=half):
                    acc = None
                    for t in range(terms):
                        term = mm(turned[side * terms + t], n_refs[p * terms + t][0])
                        acc = term if acc is None else acc + term
                    acc = acc.astype(BF16)
                    for to in range(count):
                        q = order_b[to] if half else to
                        out = outs[2 * half + to // cut]
                        at = to % cut
                        out[at * width : (at + 1) * width, :] = acc[q * width : (q + 1) * width, :]

    def n_spec(p, lead):
        last = starts[p + 1] - starts[p] - 1
        return pl.BlockSpec((1, rows, tile), lambda j, _: (lead, 0, jnp.clip(j - starts[p], 0, last)))

    in_specs = [
        pl.BlockSpec((rows, width), lambda j, p, q=q: (0, p[q])) for _ in range(n_sides * terms) for q in range(count)
    ]
    in_specs += [n_spec(p, lead) for p, (_, n) in enumerate(parts) for _, lead in n]
    operands = [cube.places(0)] + [d for side in sides for d in side for _ in range(count)]
    operands += [a for _, n in parts for a, _ in n]
    out_a = jax.ShapeDtypeStruct((cut * width, half_steps * tile), BF16)
    out_b = jax.ShapeDtypeStruct((cut * width, (steps - half_steps) * tile), BF16)
    spec_a = pl.BlockSpec((cut * width, tile), lambda j, _: (0, jnp.minimum(j, half_steps - 1)))
    spec_b = pl.BlockSpec((cut * width, tile), lambda j, _: (0, jnp.maximum(j - half_steps, 0)))
    keep_a, send_a, keep_b, send_b = kernel_call(
        body,
        name,
        2 * terms * rows * count * width * steps * tile,
        operands,
        [out_a, out_a, out_b, out_b],
        grid_spec=pltpu.PrefetchScalarGridSpec(
            num_scalar_prefetch=1,
            grid=(steps,),
            in_specs=in_specs,
            out_specs=[spec_a, spec_a, spec_b, spec_b],
            scratch_shapes=[pltpu.VMEM((n_sides * terms, count * width, rows), BF16)],
        ),
    )
    return (keep_a, send_a), (keep_b, send_b)


def head_columns(heads, kv):
    keys, values = heads * HEAD_DIM, (heads + kv) * HEAD_DIM
    for h in range(heads):
        c = h // (heads // kv)
        yield (
            slice(h * HEAD_DIM, (h + 1) * HEAD_DIM),
            slice(keys + c * HEAD_DIM, keys + (c + 1) * HEAD_DIM),
            slice(values + c * HEAD_DIM, values + (c + 1) * HEAD_DIM),
        )


def segments(ends_ref, count, place):
    found = jnp.zeros_like(place)
    for i in range(count):
        found += (ends_ref[i] <= place).astype(jnp.int32)
    return found


def allowed_pairs(ends_ref, count, j, block, rows):
    query = j * block + lax.broadcasted_iota(jnp.int32, (block, 128), 0)
    key = lax.broadcasted_iota(jnp.int32, (8, rows), 1)
    query_segment, key_segment = segments(ends_ref, count, query)[:, :1], segments(ends_ref, count, key)[:1]
    return (query_segment == key_segment) & (key[:1] <= query[:, :1])


def turn_heads(read, write, columns, cosine, sine):
    step = 2 * HEAD_DIM
    for at in range(0, columns, step):
        cut = slice(at, min(at + step, columns))
        write(cut, turned(read(cut), cosine, sine).astype(BF16))


def attention_forward(ends, owners, x_blocks, gain, w, skip, table, heads, kv):
    blocks = len(x_blocks)
    own_rows, features = x_blocks[0].shape
    rows, width = own_rows * blocks, w.shape[1] - skip
    tile = math.gcd(math.gcd(width, skip), 256)
    steps = width // tile
    block = tile_of(rows, 256)
    turn_width = (heads + kv) * HEAD_DIM
    at_sine = table.shape[1] // 2
    scale = 1.0 / math.sqrt(HEAD_DIM)

    def body(ends_ref, owners_ref, *refs):
        x_refs, (gain_ref, w_ref, table_ref, h_ref, low_ref, out_ref, mass_ref, qkv) = refs[:blocks], refs[blocks:]
        step = pl.program_id(0)

        @pl.when(step == 0)
        def _():
            for r in range(blocks):
                normed, _ = norm_parts(x_refs[r][...].astype(F32))
                at = pl.multiple_of(owners_ref[r] * own_rows, own_rows)
                h_ref[pl.ds(at, own_rows), :] = (normed * gain_ref[...]).astype(BF16)

        for k in range(steps):

            @pl.when(step == k)
            def _(k=k):
                qkv[:, k * tile : (k + 1) * tile] = mm(h_ref[...], w_ref[...])

        @pl.when(step == steps)
        def _():
            def write(cut, v):
                low_ref[:, cut] = v

            turn_heads(lambda cut: qkv[:, cut], write, turn_width, table_ref[:, :at_sine], table_ref[:, at_sine:])
            low_ref[:, turn_width:] = qkv[:, turn_width:].astype(BF16)

        @pl.when(step >= steps)
        def _():
            j = step - steps
            allowed = allowed_pairs(ends_ref, ends.shape[0], j, block, rows)
            here = pl.ds(pl.multiple_of(j * block, block), block)
            lane = lax.broadcasted_iota(jnp.int32, (block, 128), 1)
            mass = jnp.zeros((block, 128), F32)
            for h, (q_at, k_at, v_at) in enumerate(head_columns(heads, kv)):
                scores = outer(low_ref[here, q_at], low_ref[:, k_at]) * scale
                scores = jnp.where(allowed, scores, -1e30)
                row_max = jnp.max(scores, axis=1, keepdims=True)
                weights = jnp.exp(scores - row_max)
                row_sum = jnp.sum(weights, axis=1, keepdims=True)
                weights_low = (weights / row_sum).astype(BF16)
                out_ref[:, q_at] = mm(weights_low, low_ref[:, v_at]).astype(BF16)
                mass = jnp.where(lane == h, row_max + jnp.log(row_sum), mass)
            mass_ref[...] = mass

    return kernel_call(
        body,
        "attention_forward",
        4 * rows * rows * heads * HEAD_DIM + 2 * rows * features * width,
        (ends, owners, *x_blocks, gain, w, table),
        (
            jax.ShapeDtypeStruct((rows, features), BF16),
            jax.ShapeDtypeStruct((rows, width), BF16),
            jax.ShapeDtypeStruct((rows, heads * HEAD_DIM), BF16),
            jax.ShapeDtypeStruct((rows, 128), F32),
        ),
        grid_spec=pltpu.PrefetchScalarGridSpec(
            num_scalar_prefetch=2,
            grid=(steps + rows // block,),
            in_specs=[whole((own_rows, features))] * blocks
            + [
                whole((1, features)),
                pl.BlockSpec((features, tile), lambda j, *_: (0, skip // tile + jnp.minimum(j, steps - 1))),
                whole(table.shape),
            ],
            out_specs=[
                whole((rows, features)),
                whole((rows, width)),
                pl.BlockSpec((block, heads * HEAD_DIM), lambda j, *_: (jnp.maximum(j - steps, 0), 0)),
                pl.BlockSpec((block, 128), lambda j, *_: (jnp.maximum(j - steps, 0), 0)),
            ],
            scratch_shapes=[pltpu.VMEM((rows, width), F32)],
        ),
    )


def attention_backward(ends, grad_rows, w, low, mass, table, heads, kv):
    rows, features = grad_rows.shape
    width, out_width = low.shape[1], heads * HEAD_DIM
    block = tile_of(rows, 256)
    scale = 1.0 / math.sqrt(HEAD_DIM)

    at_sine = table.shape[1] // 2

    def body(ends_ref, grad_ref, w_ref, low_ref, mass_ref, table_ref, out_ref, low_grad, q_grad, k_grad, v_grad):
        j = pl.program_id(0)

        @pl.when(j == 0)
        def _():
            low_grad[...] = mm(grad_ref[...], w_ref[...]).astype(BF16)
            k_grad[...] = jnp.zeros_like(k_grad)
            v_grad[...] = jnp.zeros_like(v_grad)

        allowed = allowed_pairs(ends_ref, ends.shape[0], j, block, rows)
        here = pl.ds(pl.multiple_of(j * block, block), block)
        for h, (q_at, k_at, v_at) in enumerate(head_columns(heads, kv)):
            query, grad = low_ref[here, q_at], low_grad[here, q_at]
            scores = outer(query, low_ref[:, k_at]) * scale
            probs = jnp.exp(jnp.where(allowed, scores, -1e30) - mass_ref[:, h : h + 1])
            grad_probs = outer(grad, low_ref[:, v_at])
            delta = jnp.sum(probs * grad_probs, axis=1, keepdims=True)
            grad_scores = (probs * (grad_probs - delta)).astype(BF16)
            q_grad[:, q_at] = mm(grad_scores, low_ref[:, k_at]) * scale
            c = h // (heads // kv)
            kv_at = slice(c * HEAD_DIM, (c + 1) * HEAD_DIM)
            k_grad[:, kv_at] += inner(grad_scores, query)
            v_grad[:, kv_at] += inner(probs.astype(BF16), grad)

        def write_q(cut, v):
            out_ref[here, cut] = v

        def write_k(cut, v):
            out_ref[:, out_width + cut.start : out_width + cut.stop] = v

        turn_heads(lambda cut: q_grad[:, cut], write_q, out_width, table_ref[here, :at_sine], -table_ref[here, at_sine:])

        @pl.when(j == pl.num_programs(0) - 1)
        def _():
            turn_heads(lambda cut: k_grad[:, cut] * scale, write_k, kv * HEAD_DIM, table_ref[:, :at_sine], -table_ref[:, at_sine:])
            out_ref[:, out_width + kv * HEAD_DIM :] = v_grad[...].astype(BF16)

    return kernel_call(
        body,
        "attention_backward",
        10 * rows * rows * heads * HEAD_DIM + 2 * rows * features * out_width,
        (ends, grad_rows, w, low, mass, table),
        jax.ShapeDtypeStruct((rows, width), BF16),
        grid_spec=pltpu.PrefetchScalarGridSpec(
            num_scalar_prefetch=1,
            grid=(rows // block,),
            in_specs=[
                whole((rows, features)),
                pl.BlockSpec((features, out_width), lambda j, _: (0, 0)),
                whole((rows, width)),
                pl.BlockSpec((block, 128), lambda j, _: (j, 0)),
                whole(table.shape),
            ],
            out_specs=whole((rows, width)),
            scratch_shapes=[
                pltpu.VMEM((rows, out_width), BF16),
                pltpu.VMEM((block, out_width), F32),
                pltpu.VMEM((rows, kv * HEAD_DIM), F32),
                pltpu.VMEM((rows, kv * HEAD_DIM), F32),
            ],
        ),
    )


def per_device(
    dp_size,
    tensor_size,
    tokens,
    seq_lengths,
    seq_group,
    attn_gain,
    w_query,
    w_key,
    w_value,
    w_out,
    mlp_gain,
    w_gate,
    w_up,
    w_down,
    cotangent,
):
    cube = Cube(dp_size)
    line = Line(tensor_size)
    width_q, width_k = w_query.shape[1], w_key.shape[1]
    own_rows = tokens.shape[0]
    row_count = own_rows * tensor_size

    width_out, units = w_out.shape[0], w_gate.shape[1]

    rows_all = line.gather(tokens)
    gains = cube.gather_columns(jnp.stack([attn_gain, mlp_gain])).astype(F32)
    gain_one, gain_two = gains[:1], gains[1:]
    w_attn = lax.all_gather(jnp.concatenate([w_out.T, w_query, w_key, w_value], axis=1), "dp", axis=0, tiled=True)
    w_mlp = lax.all_gather(jnp.concatenate([w_gate, w_up, w_down.T], axis=1), "dp", axis=0, tiled=True)
    incoming_blocks = line.gather(after(cotangent, *rows_all))

    order = Order()
    heads_here = width_q // HEAD_DIM
    kv_here = width_k // HEAD_DIM
    ends, position = layout(seq_lengths, seq_group, cube.me, row_count)
    table = order(lambda p: rope_tables(p, HEAD_DIM), position)
    attn_input, low_qkv, attended, log_mass = order(
        lambda e, x, g, w, t: attention_forward(e, line.owners, x, g, w, width_out, t, heads_here, kv_here),
        ends,
        rows_all,
        gain_one,
        w_attn,
        table,
    )
    attn_input_other = cube.swap(attn_input, 1)
    tokens_f = tokens.astype(F32)
    normed_one, factor_one = norm_parts(tokens_f)
    out_parts = order(
        lambda a, w: rows_product(a, [0], w, 0, "attention_out", line.owners),
        after(attended, incoming_blocks[1])[None],
        w_attn,
    )
    attended_other = cube.swap(attended, 1)
    residual = order(lambda x, *terms: x + total32(terms), tokens_f, *line.scatter(out_parts))
    normed_two, factor_two = norm_parts(residual)
    mlp_blocks = line.gather((normed_two * gain_two).astype(BF16))

    mlp_input, incoming, unit_grads = order(
        lambda h, c, w: feed_forward(h, c, w, line.owners),
        mlp_blocks,
        incoming_blocks,
        after(w_mlp, attn_input_other, attended_other),
    )
    mlp_others = [cube.swap(v, 1) for v in (mlp_input, incoming, unit_grads)]
    two_parts = order(lambda a, w: rows_product(a, [0, 1], w, 0, "feed_forward_rows_grad"), unit_grads, w_mlp)
    two_sum = lax.psum_scatter(two_parts, "tensor", scatter_dimension=0, tiled=True)

    def mlp_grad(h, c, n, h_other, c_other, n_other):
        parts = [(side, [(n, lead), (n_other, lead)]) for side, lead in ((0, 0), (0, 1), (1, 2))]
        return weight_grad([[h, h_other], [c, c_other]], parts, cube, 512, "feed_forward_grad")

    mlp_pairs = cube.first_hop(order(mlp_grad, mlp_input, incoming, unit_grads, *mlp_others))
    grad_residual = order(
        lambda c, g, n, f, t: c.astype(F32) + norm_back(t.astype(F32), g, n, f),
        cotangent,
        gain_two,
        normed_two,
        factor_two,
        two_sum,
    )
    grad_attn_rows = lax.all_gather(grad_residual.astype(BF16), "tensor", axis=0, tiled=True)
    block_parts = order(lambda a, w: rows_product(a, [2], w, 2 * units, "block_out"), unit_grads, w_mlp)
    block_parts, grad_attn_rows = lax.optimization_barrier((block_parts, grad_attn_rows))
    block_sum = lax.psum_scatter(block_parts, "tensor", scatter_dimension=0, tiled=True)
    rows_other = cube.swap(grad_attn_rows, 1)

    grad_qkv = order(
        lambda *a: attention_backward(*a, heads_here, kv_here), ends, grad_attn_rows, w_attn, low_qkv, log_mass, table
    )
    mlp_terms = cube.other_hops(mlp_pairs, order)
    one_parts = order(
        lambda a, w: rows_product(a, [0], w, width_out, "attention_rows_grad"), grad_qkv[None], w_attn
    )
    one_sum = lax.psum_scatter(after(one_parts, block_sum), "tensor", scatter_dimension=0, tiled=True)


    def attn_grad(y, y_other, h, h_other, a, a_other, g, g_other):
        parts = [(0, [(a[None], 0), (a_other[None], 0)]), (1, [(g[None], 0), (g_other[None], 0)])]
        return weight_grad([[y, y_other], [h, h_other]], parts, cube, 256, "attention_grad")

    attn_pairs = cube.first_hop(
        order(
            attn_grad,
            grad_attn_rows,
            rows_other,
            attn_input,
            attn_input_other,
            attended,
            attended_other,
            grad_qkv,
            cube.swap(grad_qkv, 1),
        )
    )
    block_out = order(lambda x, t: (x + t.astype(F32)).astype(BF16), residual, block_sum)
    attn_terms = cube.other_hops(attn_pairs, order)

    def gain_terms(*pairs):
        return functools.reduce(lambda a, b: a + b, [jnp.sum(w.astype(F32) * g, axis=1) for w, g in pairs])

    def mlp_finals(terms, gate, up):
        sums = block_sum32(terms)
        gate_grad, up_grad, down_grad = sums[:, :units], sums[:, units : 2 * units], sums[:, 2 * units :].T
        return gain_terms((gate, gate_grad), (up, up_grad)), gate_grad, up_grad, down_grad

    mlp_gain_terms, gate_grad, up_grad, down_grad = order(mlp_finals, mlp_terms, w_gate, w_up)
    grad_tokens = order(
        lambda c, g, n, f, t: (c + norm_back(t.astype(F32), g, n, f)).astype(BF16),
        grad_residual,
        gain_one,
        normed_one,
        factor_one,
        one_sum,
    )
    attn_sum = block_sum32(attn_terms)
    out_grad, qkv_grad = attn_sum[:, :width_out].T, attn_sum[:, width_out:]
    query_grad = qkv_grad[:, :width_q]
    key_grad = qkv_grad[:, width_q : width_q + width_k]
    value_grad = qkv_grad[:, width_q + width_k :]
    attn_gain_terms = gain_terms((w_query, query_grad), (w_key, key_grad), (w_value, value_grad))
    gain_sums = line.total(jnp.stack([attn_gain_terms, mlp_gain_terms]))
    attn_gain_grad = gain_sums[0] / attn_gain.astype(F32)
    mlp_gain_grad = gain_sums[1] / mlp_gain.astype(F32)
    return (
        block_out,
        grad_tokens,
        attn_gain_grad,
        query_grad,
        key_grad,
        value_grad,
        out_grad,
        mlp_gain_grad,
        gate_grad,
        up_grad,
        down_grad,
    )


def solution(mesh):
    return jax.shard_map(
        functools.partial(per_device, mesh.shape["dp"], mesh.shape["tensor"]),
        mesh=mesh,
        in_specs=(
            P(("dp", "tensor"), None),
            P(),
            P(),
            P("dp"),
            P("dp", "tensor"),
            P("dp", "tensor"),
            P("dp", "tensor"),
            P("tensor", "dp"),
            P("dp"),
            P("dp", "tensor"),
            P("dp", "tensor"),
            P("tensor", "dp"),
            P(("dp", "tensor"), None),
        ),
        out_specs=(
            P(("dp", "tensor"), None),
            P(("dp", "tensor"), None),
            P("dp"),
            P("dp", "tensor"),
            P("dp", "tensor"),
            P("dp", "tensor"),
            P("tensor", "dp"),
            P("dp"),
            P("dp", "tensor"),
            P("dp", "tensor"),
            P("tensor", "dp"),
        ),
        check_vma=False,
    )
```

```python
import functools
import math

import jax
import jax.numpy as jnp
from jax import lax
from jax.experimental import pallas as pl
from jax.experimental.pallas import tpu as pltpu
from jax.sharding import PartitionSpec as P

HEAD_DIM = 64
EPSILON = 1e-05
ROPE_BASE = 500000.0
F32 = jnp.float32
BF16 = jnp.bfloat16


def rope_tables(position, width):
    half_width = width // 2
    steps_f = jnp.arange(half_width, dtype=F32)
    inverse = 1.0 / ROPE_BASE ** (steps_f * 2.0 / width)
    angles = position.astype(F32)[:, None] * inverse[None, :]
    cosine, sine = jnp.cos(angles), jnp.sin(angles)
    return jnp.concatenate([cosine] * 4 + [-sine, sine] * 2, axis=1)


def turned(values, cosine, sine):
    width = values.shape[1]
    half = HEAD_DIM // 2
    lane = lax.broadcasted_iota(jnp.int32, values.shape, 1)
    if width > HEAD_DIM:
        up, down = pltpu.roll(values, half, axis=1), pltpu.roll(values, width - half, axis=1)
        swapped = jnp.where(lane % HEAD_DIM < half, down, up)
    else:
        swapped = jnp.concatenate([values[:, half:], values[:, :half]], axis=1)
    return values * cosine[:, :width] + swapped * sine[:, :width]


def layout(seq_lengths, seq_group, group_id, row_count):
    owned = seq_group == group_id
    owned_len = jnp.where(owned, seq_lengths, 0)
    ends = jnp.where(owned, jnp.cumsum(owned_len), row_count + 1)
    row = jnp.arange(row_count, dtype=jnp.int32)
    offsets = jnp.sum((ends[None, :] <= row[:, None]).astype(jnp.int32) * owned_len[None, :], axis=1)
    return (ends.astype(jnp.int32), row - offsets)


def mm(left, right):
    return jnp.dot(left, right, preferred_element_type=F32)


def inner(left, right):
    return lax.dot_general(left, right, (((0,), (0,)), ((), ())), preferred_element_type=F32)


def outer(left, right):
    return lax.dot_general(left, right, (((1,), (1,)), ((), ())), preferred_element_type=F32)


def norm_parts(values):
    factor = lax.rsqrt(jnp.mean(values * values, axis=-1, keepdims=True) + EPSILON)
    return (values * factor, factor)


def norm_back(grad_rows, gain, normed, factor):
    scaled = grad_rows * gain
    return factor * (scaled - normed * jnp.mean(scaled * normed, axis=-1, keepdims=True))


def after(value, *deps):
    return lax.optimization_barrier((value,) + deps)[0]


class Line:
    def __init__(self, size):
        self.size = size
        self.index = lax.axis_index("tensor")
        self.owners = lax.rem(self.index - jnp.arange(size, dtype=jnp.int32) + size, size)

    def shift(self, v, r):
        return lax.ppermute(v, "tensor", [(i, (i + r) % self.size) for i in range(self.size)])

    def gather(self, v):
        return [v] + [self.shift(v, r) for r in range(1, self.size)]

    def scatter(self, parts):
        return [parts[0]] + [self.shift(parts[r], -r) for r in range(1, self.size)]

    def total(self, v):
        return functools.reduce(lambda a, b: a + b, [v] + [self.shift(v, r) for r in range(1, self.size)])


class Cube:
    def __init__(self, size):
        self.size = size
        self.me = lax.axis_index("dp")
        self.bits = [1 << b for b in range(size.bit_length() - 1)]

    def swap(self, v, m):
        return lax.ppermute(v, "dp", [(i, i ^ m) for i in range(self.size)])

    def gather_columns(self, v):
        for m in self.bits:
            other = self.swap(v, m)
            both = jnp.concatenate([v, other], axis=1), jnp.concatenate([other, v], axis=1)
            v = jnp.where((self.me & m) == 0, *both)
        return v

    def places(self, half):
        count = self.size // 2
        bits = self.hops(half)
        keys = [0]
        for m in reversed(bits):
            keys = keys + [k | m for k in keys]
        return self.me ^ jnp.array(keys[:count], jnp.int32)

    def hops(self, half):
        return self.bits[1:] if half else self.bits[:0:-1]

    def first_hop(self, pairs):
        return [(keep, self.swap(send, self.hops(half)[0])) for half, (keep, send) in enumerate(pairs)]

    def other_hops(self, pairs, order):
        terms = [list(pair) for pair in pairs]
        for hop in range(1, len(self.bits) - 1):
            rows = terms[0][-1].shape[0]
            sent = order(lambda *p: [total32([t[rows // 2 : rows] for t in ts]).astype(BF16) for ts in p], *terms)
            for half in range(2):
                terms[half].append(self.swap(sent[half], self.hops(half)[hop]))
        return terms


class Order:
    def __init__(self):
        self.last = None

    def __call__(self, step, *args):
        if self.last is not None:
            args, _ = lax.optimization_barrier((args, self.last))
        out = step(*args)
        self.last = jax.tree.leaves(out)[0]
        return out


def block_sum32(halves):
    return jnp.concatenate([total32([t[: terms[-1].shape[0]] for t in terms]) for terms in halves], axis=1)


def total32(terms):
    return functools.reduce(lambda a, b: a + b, [t.astype(F32) for t in terms])


def tile_of(size, most):
    while size % most:
        most //= 2
    return most


def kernel_call(body, name, flops, operands, out_shape, vmem=48, **kwargs):
    shapes = jax.tree.leaves(out_shape)
    moved = sum(math.prod(a.shape) * a.dtype.itemsize for a in list(operands) + shapes)
    return pl.pallas_call(
        body,
        out_shape=out_shape,
        name=name,
        cost_estimate=pl.CostEstimate(flops=flops, bytes_accessed=moved, transcendentals=0),
        compiler_params=pltpu.CompilerParams(vmem_limit_bytes=vmem << 20),
        **kwargs,
    )(*operands)


def whole(shape):
    return pl.BlockSpec(shape, lambda *_: (0,) * len(shape))


def norm_backward(base, gain, x, grad, keep):
    rows, features = x.shape
    block = tile_of(rows, 64)

    def body(base_ref, gain_ref, x_ref, grad_ref, low_ref, *wide_ref):
        normed, factor = norm_parts(x_ref[...].astype(F32))
        total = base_ref[...].astype(F32) + norm_back(grad_ref[...].astype(F32), gain_ref[...], normed, factor)
        low_ref[...] = total.astype(BF16)
        if keep:
            wide_ref[0][...] = total

    spec = pl.BlockSpec((block, features), lambda j: (j, 0))
    kinds = (BF16, F32) if keep else (BF16,)
    return kernel_call(
        body,
        "norm_backward",
        20 * rows * features,
        (base, gain, x, grad),
        [jax.ShapeDtypeStruct((rows, features), kind) for kind in kinds],
        grid=(rows // block,),
        in_specs=[spec, whole((1, features)), spec, spec],
        out_specs=[spec] * len(kinds),
    )


def feed_forward(h_blocks, c_blocks, w, owners):
    count = len(h_blocks)
    rows, features = h_blocks[0].shape
    units = w.shape[1] // 3
    tile = tile_of(units, 256)
    steps = units // tile

    def body(owners_ref, *refs):
        h_refs, c_refs = refs[:count], refs[count : 2 * count]
        gate_ref, up_ref, down_ref, h_all, c_all, out_ref = refs[2 * count :]

        @pl.when(pl.program_id(0) == 0)
        def _():
            for r in range(count):
                at = pl.multiple_of(owners_ref[r] * rows, rows)
                h_all[pl.ds(at, rows), :] = h_refs[r][...]
                c_all[pl.ds(at, rows), :] = c_refs[r][...]

        gate = mm(h_all[...], gate_ref[...])
        up = mm(h_all[...], up_ref[...])
        grad_hidden = mm(c_all[...], down_ref[...])
        sig = 1.0 / (1.0 + jnp.exp(-gate))
        silu = gate * sig
        out_ref[0] = (grad_hidden * up * (sig * (1.0 + gate * (1.0 - sig)))).astype(BF16)
        out_ref[1] = (grad_hidden * silu).astype(BF16)
        out_ref[2] = (silu * up).astype(BF16)

    total = rows * count
    wide = jax.ShapeDtypeStruct((total, features), BF16)
    return kernel_call(
        body,
        "feed_forward",
        6 * total * features * units,
        (owners, *h_blocks, *c_blocks, w, w, w),
        (wide, wide, jax.ShapeDtypeStruct((3, total, units), BF16)),
        grid_spec=pltpu.PrefetchScalarGridSpec(
            num_scalar_prefetch=1,
            grid=(steps,),
            in_specs=[whole((rows, features))] * (2 * count)
            + [pl.BlockSpec((features, tile), lambda j, _, k=k: (0, k * steps + j)) for k in range(3)],
            out_specs=[whole((total, features))] * 2 + [pl.BlockSpec((3, total, tile), lambda j, _: (0, 0, j))],
        ),
    )


def rows_product(a, leads, w, first, name, owners=None):
    rows, units = a.shape[1:]
    features = w.shape[0]
    tile = tile_of(features, 512 if units * len(leads) > 1024 else 1024)
    count = 1 if owners is None else owners.shape[0]
    block = rows // count
    width = units * len(leads)
    aligned = first % width == 0

    def body(owners_ref, *refs):
        a_refs, w_ref, outs, turned = refs[: len(leads)], refs[len(leads)], refs[len(leads) + 1 : -1], refs[-1]
        if owners is not None:

            @pl.when(pl.program_id(0) == 0)
            def _():
                for r in range(count):
                    at = pl.multiple_of(owners_ref[r] * block, block)
                    for k in range(len(leads)):
                        turned[k, r * block : (r + 1) * block, :] = a_refs[k][0, pl.ds(at, block), :]

        at = 0 if aligned else first
        acc = None
        for k, a_ref in enumerate(a_refs):
            term = outer(a_ref[0] if owners is None else turned[k], w_ref[:, at : at + units])
            acc = term if acc is None else acc + term
            at += units
        for r in range(count):
            outs[r][...] = acc[r * block : (r + 1) * block, :].astype(BF16)

    spec = pl.BlockSpec((tile, width), lambda j, _: (j, first // width))
    if not aligned:
        spec = pl.BlockSpec((tile, w.shape[1]), lambda j, _: (j, 0))
    outs = kernel_call(
        body,
        name,
        2 * rows * features * width,
        [jnp.zeros((1,), jnp.int32) if owners is None else owners] + [a] * len(leads) + [w],
        [jax.ShapeDtypeStruct((block, features), BF16)] * count,
        grid_spec=pltpu.PrefetchScalarGridSpec(
            num_scalar_prefetch=1,
            grid=(features // tile,),
            in_specs=[pl.BlockSpec((1, rows, units), lambda j, _, k=k: (k, 0, 0)) for k in leads] + [spec],
            out_specs=[pl.BlockSpec((block, tile), lambda j, _: (0, j))] * count,
            scratch_shapes=[pltpu.VMEM((len(leads), rows, units) if owners is not None else (1, 16, 128), BF16)],
        ),
    )
    return outs[0] if owners is None else outs


def weight_grad(sides, parts, cube, most, name):
    terms = len(sides[0])
    rows, width = sides[0][0].shape[0], sides[0][0].shape[1] // cube.size
    count = cube.size // 2
    sizes = [n[0][0].shape[-1] for _, n in parts]
    tile = functools.reduce(math.gcd, sizes, most)
    starts = [0]
    for size in sizes:
        starts.append(starts[-1] + size // tile)
    n_sides, n_parts, steps = len(sides), len(parts), starts[-1]
    half_steps = (steps + 1) // 2
    bounds = [0, half_steps, steps]
    place_a, place_b = ([0], [0])
    for m in reversed(cube.hops(0)):
        place_a = place_a + [k | m for k in place_a]
    for m in reversed(cube.hops(1)):
        place_b = place_b + [k | m for k in place_b]
    order_b = [place_a.index(k) for k in place_b]
    cut = count // 2

    def body(places_ref, *refs):
        d_refs = refs[: n_sides * terms * count]
        n_refs = refs[n_sides * terms * count :][: n_parts * terms]
        outs, turned = refs[-5:-1], refs[-1]
        j = pl.program_id(0)

        @pl.when(j == 0)
        def _():
            for k in range(n_sides * terms):
                for q in range(count):
                    turned[k, q * width : (q + 1) * width, :] = d_refs[k * count + q][...].T

        for p, (side, _) in enumerate(parts):
            for half in range(2):
                first, last = max(starts[p], bounds[half]), min(starts[p + 1], bounds[half + 1])
                if first >= last:
                    continue

                @pl.when((j >= first) & (j < last))
                def _(p=p, side=side, half=half):
                    acc = None
                    for t in range(terms):
                        term = mm(turned[side * terms + t], n_refs[p * terms + t][0])
                        acc = term if acc is None else acc + term
                    acc = acc.astype(BF16)
                    for to in range(count):
                        q = order_b[to] if half else to
                        out = outs[2 * half + to // cut]
                        at = to % cut
                        out[at * width : (at + 1) * width, :] = acc[q * width : (q + 1) * width, :]

    def n_spec(p, lead):
        last = starts[p + 1] - starts[p] - 1
        return pl.BlockSpec((1, rows, tile), lambda j, _: (lead, 0, jnp.clip(j - starts[p], 0, last)))

    in_specs = [
        pl.BlockSpec((rows, width), lambda j, p, q=q: (0, p[q])) for _ in range(n_sides * terms) for q in range(count)
    ]
    in_specs += [n_spec(p, lead) for p, (_, n) in enumerate(parts) for _, lead in n]
    operands = [cube.places(0)] + [d for side in sides for d in side for _ in range(count)]
    operands += [a for _, n in parts for a, _ in n]
    out_a = jax.ShapeDtypeStruct((cut * width, half_steps * tile), BF16)
    out_b = jax.ShapeDtypeStruct((cut * width, (steps - half_steps) * tile), BF16)
    spec_a = pl.BlockSpec((cut * width, tile), lambda j, _: (0, jnp.minimum(j, half_steps - 1)))
    spec_b = pl.BlockSpec((cut * width, tile), lambda j, _: (0, jnp.maximum(j - half_steps, 0)))
    keep_a, send_a, keep_b, send_b = kernel_call(
        body,
        name,
        2 * terms * rows * count * width * steps * tile,
        operands,
        [out_a, out_a, out_b, out_b],
        grid_spec=pltpu.PrefetchScalarGridSpec(
            num_scalar_prefetch=1,
            grid=(steps,),
            in_specs=in_specs,
            out_specs=[spec_a, spec_a, spec_b, spec_b],
            scratch_shapes=[pltpu.VMEM((n_sides * terms, count * width, rows), BF16)],
        ),
    )
    return (keep_a, send_a), (keep_b, send_b)


def head_columns(heads, kv):
    keys, values = heads * HEAD_DIM, (heads + kv) * HEAD_DIM
    for h in range(heads):
        c = h // (heads // kv)
        yield (
            slice(h * HEAD_DIM, (h + 1) * HEAD_DIM),
            slice(keys + c * HEAD_DIM, keys + (c + 1) * HEAD_DIM),
            slice(values + c * HEAD_DIM, values + (c + 1) * HEAD_DIM),
        )


def segments(ends_ref, count, place):
    found = jnp.zeros_like(place)
    for i in range(count):
        found += (ends_ref[i] <= place).astype(jnp.int32)
    return found


def allowed_pairs(ends_ref, count, j, block, rows):
    query = j * block + lax.broadcasted_iota(jnp.int32, (block, 128), 0)
    key = lax.broadcasted_iota(jnp.int32, (8, rows), 1)
    query_segment, key_segment = segments(ends_ref, count, query)[:, :1], segments(ends_ref, count, key)[:1]
    return (query_segment == key_segment) & (key[:1] <= query[:, :1])


def turn_heads(read, write, columns, cosine, sine):
    step = 2 * HEAD_DIM
    for at in range(0, columns, step):
        cut = slice(at, min(at + step, columns))
        write(cut, turned(read(cut), cosine, sine).astype(BF16))


def attention_forward(ends, owners, x_blocks, gain, w, skip, table, heads, kv):
    blocks = len(x_blocks)
    own_rows, features = x_blocks[0].shape
    rows, width = own_rows * blocks, w.shape[1] - skip
    tile = math.gcd(math.gcd(width, skip), 256)
    steps = width // tile
    block = tile_of(rows, 256)
    turn_width = (heads + kv) * HEAD_DIM
    at_sine = table.shape[1] // 2
    scale = 1.0 / math.sqrt(HEAD_DIM)

    def body(ends_ref, owners_ref, *refs):
        x_refs, (gain_ref, w_ref, table_ref, h_ref, low_ref, out_ref, mass_ref, qkv) = refs[:blocks], refs[blocks:]
        step = pl.program_id(0)

        @pl.when(step == 0)
        def _():
            for r in range(blocks):
                normed, _ = norm_parts(x_refs[r][...].astype(F32))
                at = pl.multiple_of(owners_ref[r] * own_rows, own_rows)
                h_ref[pl.ds(at, own_rows), :] = (normed * gain_ref[...]).astype(BF16)

        for k in range(steps):

            @pl.when(step == k)
            def _(k=k):
                qkv[:, k * tile : (k + 1) * tile] = mm(h_ref[...], w_ref[...])

        @pl.when(step == steps)
        def _():
            def write(cut, v):
                low_ref[:, cut] = v

            turn_heads(lambda cut: qkv[:, cut], write, turn_width, table_ref[:, :at_sine], table_ref[:, at_sine:])
            low_ref[:, turn_width:] = qkv[:, turn_width:].astype(BF16)

        @pl.when(step >= steps)
        def _():
            j = step - steps
            allowed = allowed_pairs(ends_ref, ends.shape[0], j, block, rows)
            here = pl.ds(pl.multiple_of(j * block, block), block)
            lane = lax.broadcasted_iota(jnp.int32, (block, 128), 1)
            mass = jnp.zeros((block, 128), F32)
            for h, (q_at, k_at, v_at) in enumerate(head_columns(heads, kv)):
                scores = outer(low_ref[here, q_at], low_ref[:, k_at]) * scale
                scores = jnp.where(allowed, scores, -1e30)
                row_max = jnp.max(scores, axis=1, keepdims=True)
                weights = jnp.exp(scores - row_max)
                row_sum = jnp.sum(weights, axis=1, keepdims=True)
                weights_low = (weights / row_sum).astype(BF16)
                out_ref[:, q_at] = mm(weights_low, low_ref[:, v_at]).astype(BF16)
                mass = jnp.where(lane == h, row_max + jnp.log(row_sum), mass)
            mass_ref[...] = mass

    return kernel_call(
        body,
        "attention_forward",
        4 * rows * rows * heads * HEAD_DIM + 2 * rows * features * width,
        (ends, owners, *x_blocks, gain, w, table),
        (
            jax.ShapeDtypeStruct((rows, features), BF16),
            jax.ShapeDtypeStruct((rows, width), BF16),
            jax.ShapeDtypeStruct((rows, heads * HEAD_DIM), BF16),
            jax.ShapeDtypeStruct((rows, 128), F32),
        ),
        grid_spec=pltpu.PrefetchScalarGridSpec(
            num_scalar_prefetch=2,
            grid=(steps + rows // block,),
            in_specs=[whole((own_rows, features))] * blocks
            + [
                whole((1, features)),
                pl.BlockSpec((features, tile), lambda j, *_: (0, skip // tile + jnp.minimum(j, steps - 1))),
                whole(table.shape),
            ],
            out_specs=[
                whole((rows, features)),
                whole((rows, width)),
                pl.BlockSpec((block, heads * HEAD_DIM), lambda j, *_: (jnp.maximum(j - steps, 0), 0)),
                pl.BlockSpec((block, 128), lambda j, *_: (jnp.maximum(j - steps, 0), 0)),
            ],
            scratch_shapes=[pltpu.VMEM((rows, width), F32)],
        ),
    )


def attention_backward(ends, grad_rows, w, low, mass, table, heads, kv):
    rows, features = grad_rows.shape
    width, out_width = low.shape[1], heads * HEAD_DIM
    block = tile_of(rows, 256)
    scale = 1.0 / math.sqrt(HEAD_DIM)

    at_sine = table.shape[1] // 2

    def body(ends_ref, grad_ref, w_ref, low_ref, mass_ref, table_ref, out_ref, low_grad, q_grad, k_grad, v_grad):
        j = pl.program_id(0)

        @pl.when(j == 0)
        def _():
            low_grad[...] = mm(grad_ref[...], w_ref[...]).astype(BF16)
            k_grad[...] = jnp.zeros_like(k_grad)
            v_grad[...] = jnp.zeros_like(v_grad)

        allowed = allowed_pairs(ends_ref, ends.shape[0], j, block, rows)
        here = pl.ds(pl.multiple_of(j * block, block), block)
        for h, (q_at, k_at, v_at) in enumerate(head_columns(heads, kv)):
            query, grad = low_ref[here, q_at], low_grad[here, q_at]
            scores = outer(query, low_ref[:, k_at]) * scale
            probs = jnp.exp(jnp.where(allowed, scores, -1e30) - mass_ref[:, h : h + 1])
            grad_probs = outer(grad, low_ref[:, v_at])
            delta = jnp.sum(probs * grad_probs, axis=1, keepdims=True)
            grad_scores = (probs * (grad_probs - delta)).astype(BF16)
            q_grad[:, q_at] = mm(grad_scores, low_ref[:, k_at]) * scale
            c = h // (heads // kv)
            kv_at = slice(c * HEAD_DIM, (c + 1) * HEAD_DIM)
            k_grad[:, kv_at] += inner(grad_scores, query)
            v_grad[:, kv_at] += inner(probs.astype(BF16), grad)

        def write_q(cut, v):
            out_ref[here, cut] = v

        def write_k(cut, v):
            out_ref[:, out_width + cut.start : out_width + cut.stop] = v

        turn_heads(lambda cut: q_grad[:, cut], write_q, out_width, table_ref[here, :at_sine], -table_ref[here, at_sine:])

        @pl.when(j == pl.num_programs(0) - 1)
        def _():
            turn_heads(lambda cut: k_grad[:, cut] * scale, write_k, kv * HEAD_DIM, table_ref[:, :at_sine], -table_ref[:, at_sine:])
            out_ref[:, out_width + kv * HEAD_DIM :] = v_grad[...].astype(BF16)

    return kernel_call(
        body,
        "attention_backward",
        10 * rows * rows * heads * HEAD_DIM + 2 * rows * features * out_width,
        (ends, grad_rows, w, low, mass, table),
        jax.ShapeDtypeStruct((rows, width), BF16),
        grid_spec=pltpu.PrefetchScalarGridSpec(
            num_scalar_prefetch=1,
            grid=(rows // block,),
            in_specs=[
                whole((rows, features)),
                pl.BlockSpec((features, out_width), lambda j, _: (0, 0)),
                whole((rows, width)),
                pl.BlockSpec((block, 128), lambda j, _: (j, 0)),
                whole(table.shape),
            ],
            out_specs=whole((rows, width)),
            scratch_shapes=[
                pltpu.VMEM((rows, out_width), BF16),
                pltpu.VMEM((block, out_width), F32),
                pltpu.VMEM((rows, kv * HEAD_DIM), F32),
                pltpu.VMEM((rows, kv * HEAD_DIM), F32),
            ],
        ),
    )


def per_device(
    dp_size,
    tensor_size,
    tokens,
    seq_lengths,
    seq_group,
    attn_gain,
    w_query,
    w_key,
    w_value,
    w_out,
    mlp_gain,
    w_gate,
    w_up,
    w_down,
    cotangent,
):
    cube = Cube(dp_size)
    line = Line(tensor_size)
    width_q, width_k = w_query.shape[1], w_key.shape[1]
    own_rows = tokens.shape[0]
    row_count = own_rows * tensor_size

    width_out, units = w_out.shape[0], w_gate.shape[1]

    rows_all = line.gather(tokens)
    gains = cube.gather_columns(jnp.stack([attn_gain, mlp_gain])).astype(F32)
    gain_one, gain_two = gains[:1], gains[1:]
    w_attn = lax.all_gather(jnp.concatenate([w_out.T, w_query, w_key, w_value], axis=1), "dp", axis=0, tiled=True)
    w_mlp = lax.all_gather(jnp.concatenate([w_gate, w_up, w_down.T], axis=1), "dp", axis=0, tiled=True)
    incoming_blocks = line.gather(after(cotangent, *rows_all))

    order = Order()
    heads_here = width_q // HEAD_DIM
    kv_here = width_k // HEAD_DIM
    ends, position = layout(seq_lengths, seq_group, cube.me, row_count)
    table = order(lambda p: rope_tables(p, HEAD_DIM), position)
    attn_input, low_qkv, attended, log_mass = order(
        lambda e, x, g, w, t: attention_forward(e, line.owners, x, g, w, width_out, t, heads_here, kv_here),
        ends,
        rows_all,
        gain_one,
        w_attn,
        table,
    )
    attn_input_other = cube.swap(attn_input, 1)
    tokens_f = tokens.astype(F32)

    out_parts = order(
        lambda a, w: rows_product(a, [0], w, 0, "attention_out", line.owners),
        after(attended, incoming_blocks[1])[None],
        w_attn,
    )
    attended_other = cube.swap(attended, 1)
    residual = order(lambda x, *terms: x + total32(terms), tokens_f, *line.scatter(out_parts))
    normed_two, _ = norm_parts(residual)
    mlp_blocks = line.gather((normed_two * gain_two).astype(BF16))

    mlp_input, incoming, unit_grads = order(
        lambda h, c, w: feed_forward(h, c, w, line.owners),
        mlp_blocks,
        incoming_blocks,
        after(w_mlp, attn_input_other, attended_other),
    )
    mlp_others = [cube.swap(v, 1) for v in (mlp_input, incoming, unit_grads)]
    two_parts = order(lambda a, w: rows_product(a, [0, 1], w, 0, "feed_forward_rows_grad"), unit_grads, w_mlp)
    two_sum = lax.psum_scatter(two_parts, "tensor", scatter_dimension=0, tiled=True)

    def mlp_grad(h, c, n, h_other, c_other, n_other):
        parts = [(side, [(n, lead), (n_other, lead)]) for side, lead in ((0, 0), (0, 1), (1, 2))]
        return weight_grad([[h, h_other], [c, c_other]], parts, cube, 512, "feed_forward_grad")

    mlp_pairs = cube.first_hop(order(mlp_grad, mlp_input, incoming, unit_grads, *mlp_others))
    grad_low, grad_residual = order(
        lambda *a: norm_backward(*a, True), cotangent, gain_two, residual, two_sum
    )
    grad_attn_rows = lax.all_gather(grad_low, "tensor", axis=0, tiled=True)
    block_parts = order(lambda a, w: rows_product(a, [2], w, 2 * units, "block_out"), unit_grads, w_mlp)
    block_parts, grad_attn_rows = lax.optimization_barrier((block_parts, grad_attn_rows))
    block_sum = lax.psum_scatter(block_parts, "tensor", scatter_dimension=0, tiled=True)
    rows_other = cube.swap(grad_attn_rows, 1)

    grad_qkv = order(
        lambda *a: attention_backward(*a, heads_here, kv_here), ends, grad_attn_rows, w_attn, low_qkv, log_mass, table
    )
    mlp_terms = cube.other_hops(mlp_pairs, order)
    one_parts = order(
        lambda a, w: rows_product(a, [0], w, width_out, "attention_rows_grad"), grad_qkv[None], w_attn
    )
    one_sum = lax.psum_scatter(after(one_parts, block_sum), "tensor", scatter_dimension=0, tiled=True)


    def attn_grad(y, y_other, h, h_other, a, a_other, g, g_other):
        parts = [(0, [(a[None], 0), (a_other[None], 0)]), (1, [(g[None], 0), (g_other[None], 0)])]
        return weight_grad([[y, y_other], [h, h_other]], parts, cube, 256, "attention_grad")

    attn_pairs = cube.first_hop(
        order(
            attn_grad,
            grad_attn_rows,
            rows_other,
            attn_input,
            attn_input_other,
            attended,
            attended_other,
            grad_qkv,
            cube.swap(grad_qkv, 1),
        )
    )
    block_out = order(lambda x, t: (x + t.astype(F32)).astype(BF16), residual, block_sum)
    attn_terms = cube.other_hops(attn_pairs, order)

    def gain_terms(*pairs):
        return functools.reduce(lambda a, b: a + b, [jnp.sum(w.astype(F32) * g, axis=1) for w, g in pairs])

    def mlp_finals(terms, gate, up):
        sums = block_sum32(terms)
        gate_grad, up_grad, down_grad = sums[:, :units], sums[:, units : 2 * units], sums[:, 2 * units :].T
        return gain_terms((gate, gate_grad), (up, up_grad)), gate_grad, up_grad, down_grad

    mlp_gain_terms, gate_grad, up_grad, down_grad = order(mlp_finals, mlp_terms, w_gate, w_up)
    (grad_tokens,) = order(lambda *a: norm_backward(*a, False), grad_residual, gain_one, tokens, one_sum)
    attn_sum = block_sum32(attn_terms)
    out_grad, qkv_grad = attn_sum[:, :width_out].T, attn_sum[:, width_out:]
    query_grad = qkv_grad[:, :width_q]
    key_grad = qkv_grad[:, width_q : width_q + width_k]
    value_grad = qkv_grad[:, width_q + width_k :]
    attn_gain_terms = gain_terms((w_query, query_grad), (w_key, key_grad), (w_value, value_grad))
    gain_sums = line.total(jnp.stack([attn_gain_terms, mlp_gain_terms]))
    attn_gain_grad = gain_sums[0] / attn_gain.astype(F32)
    mlp_gain_grad = gain_sums[1] / mlp_gain.astype(F32)
    return (
        block_out,
        grad_tokens,
        attn_gain_grad,
        query_grad,
        key_grad,
        value_grad,
        out_grad,
        mlp_gain_grad,
        gate_grad,
        up_grad,
        down_grad,
    )


def solution(mesh):
    return jax.shard_map(
        functools.partial(per_device, mesh.shape["dp"], mesh.shape["tensor"]),
        mesh=mesh,
        in_specs=(
            P(("dp", "tensor"), None),
            P(),
            P(),
            P("dp"),
            P("dp", "tensor"),
            P("dp", "tensor"),
            P("dp", "tensor"),
            P("tensor", "dp"),
            P("dp"),
            P("dp", "tensor"),
            P("dp", "tensor"),
            P("tensor", "dp"),
            P(("dp", "tensor"), None),
        ),
        out_specs=(
            P(("dp", "tensor"), None),
            P(("dp", "tensor"), None),
            P("dp"),
            P("dp", "tensor"),
            P("dp", "tensor"),
            P("dp", "tensor"),
            P("tensor", "dp"),
            P("dp"),
            P("dp", "tensor"),
            P("dp", "tensor"),
            P("tensor", "dp"),
        ),
        check_vma=False,
    )
```

```python
import functools
import math

import jax
import jax.numpy as jnp
from jax import lax
from jax.experimental import pallas as pl
from jax.experimental.pallas import tpu as pltpu
from jax.sharding import PartitionSpec as P

HEAD_DIM = 64
EPSILON = 1e-05
ROPE_BASE = 500000.0
F32 = jnp.float32
BF16 = jnp.bfloat16


def rope_tables(position, width):
    half_width = width // 2
    steps_f = jnp.arange(half_width, dtype=F32)
    inverse = 1.0 / ROPE_BASE ** (steps_f * 2.0 / width)
    angles = position.astype(F32)[:, None] * inverse[None, :]
    cosine, sine = jnp.cos(angles), jnp.sin(angles)
    return jnp.concatenate([cosine] * 4 + [-sine, sine] * 2, axis=1)


def turned(values, cosine, sine):
    width = values.shape[1]
    half = HEAD_DIM // 2
    lane = lax.broadcasted_iota(jnp.int32, values.shape, 1)
    if width > HEAD_DIM:
        up, down = pltpu.roll(values, half, axis=1), pltpu.roll(values, width - half, axis=1)
        swapped = jnp.where(lane % HEAD_DIM < half, down, up)
    else:
        swapped = jnp.concatenate([values[:, half:], values[:, :half]], axis=1)
    return values * cosine[:, :width] + swapped * sine[:, :width]


def layout(seq_lengths, seq_group, group_id, row_count):
    owned = seq_group == group_id
    owned_len = jnp.where(owned, seq_lengths, 0)
    ends = jnp.where(owned, jnp.cumsum(owned_len), row_count + 1)
    row = jnp.arange(row_count, dtype=jnp.int32)
    offsets = jnp.sum((ends[None, :] <= row[:, None]).astype(jnp.int32) * owned_len[None, :], axis=1)
    return (ends.astype(jnp.int32), row - offsets)


def mm(left, right):
    return jnp.dot(left, right, preferred_element_type=F32)


def inner(left, right):
    return lax.dot_general(left, right, (((0,), (0,)), ((), ())), preferred_element_type=F32)


def outer(left, right):
    return lax.dot_general(left, right, (((1,), (1,)), ((), ())), preferred_element_type=F32)


def norm_parts(values):
    factor = lax.rsqrt(jnp.mean(values * values, axis=-1, keepdims=True) + EPSILON)
    return (values * factor, factor)


def norm_back(grad_rows, gain, normed, factor):
    scaled = grad_rows * gain
    return factor * (scaled - normed * jnp.mean(scaled * normed, axis=-1, keepdims=True))


def after(value, *deps):
    return lax.optimization_barrier((value,) + deps)[0]


class Line:
    def __init__(self, size):
        self.size = size
        self.index = lax.axis_index("tensor")
        self.owners = lax.rem(self.index - jnp.arange(size, dtype=jnp.int32) + size, size)

    def shift(self, v, r):
        return lax.ppermute(v, "tensor", [(i, (i + r) % self.size) for i in range(self.size)])

    def gather(self, v):
        return [v] + [self.shift(v, r) for r in range(1, self.size)]

    def scatter(self, parts):
        return [parts[0]] + [self.shift(parts[r], -r) for r in range(1, self.size)]

    def total(self, v):
        return functools.reduce(lambda a, b: a + b, [v] + [self.shift(v, r) for r in range(1, self.size)])


class Cube:
    def __init__(self, size):
        self.size = size
        self.me = lax.axis_index("dp")
        self.bits = [1 << b for b in range(size.bit_length() - 1)]

    def swap(self, v, m):
        return lax.ppermute(v, "dp", [(i, i ^ m) for i in range(self.size)])

    def gather_columns(self, v):
        for m in self.bits:
            other = self.swap(v, m)
            both = jnp.concatenate([v, other], axis=1), jnp.concatenate([other, v], axis=1)
            v = jnp.where((self.me & m) == 0, *both)
        return v

    def places(self, half):
        count = self.size // 2
        bits = self.hops(half)
        keys = [0]
        for m in reversed(bits):
            keys = keys + [k | m for k in keys]
        return self.me ^ jnp.array(keys[:count], jnp.int32)

    def hops(self, half):
        return self.bits[1:] if half else self.bits[:0:-1]

    def first_hop(self, pairs):
        return [(keep, self.swap(send, self.hops(half)[0])) for half, (keep, send) in enumerate(pairs)]

    def other_hops(self, pairs, order):
        terms = [list(pair) for pair in pairs]
        for hop in range(1, len(self.bits) - 1):
            rows = terms[0][-1].shape[0]
            sent = order(lambda *p: [total32([t[rows // 2 : rows] for t in ts]).astype(BF16) for ts in p], *terms)
            for half in range(2):
                terms[half].append(self.swap(sent[half], self.hops(half)[hop]))
        return terms


class Order:
    def __init__(self):
        self.last = None

    def __call__(self, step, *args):
        if self.last is not None:
            args, _ = lax.optimization_barrier((args, self.last))
        out = step(*args)
        self.last = jax.tree.leaves(out)[0]
        return out


def block_sum32(halves):
    return jnp.concatenate([total32([t[: terms[-1].shape[0]] for t in terms]) for terms in halves], axis=1)


def total32(terms):
    return functools.reduce(lambda a, b: a + b, [t.astype(F32) for t in terms])


def tile_of(size, most):
    while size % most:
        most //= 2
    return most


def kernel_call(body, name, flops, operands, out_shape, vmem=48, **kwargs):
    shapes = jax.tree.leaves(out_shape)
    moved = sum(math.prod(a.shape) * a.dtype.itemsize for a in list(operands) + shapes)
    return pl.pallas_call(
        body,
        out_shape=out_shape,
        name=name,
        cost_estimate=pl.CostEstimate(flops=flops, bytes_accessed=moved, transcendentals=0),
        compiler_params=pltpu.CompilerParams(vmem_limit_bytes=vmem << 20),
        **kwargs,
    )(*operands)


def whole(shape):
    return pl.BlockSpec(shape, lambda *_: (0,) * len(shape))


def norm_backward(base, gain, x, grad, keep):
    rows, features = x.shape
    block = tile_of(rows, 64)

    def body(base_ref, gain_ref, x_ref, grad_ref, low_ref, *wide_ref):
        normed, factor = norm_parts(x_ref[...].astype(F32))
        total = base_ref[...].astype(F32) + norm_back(grad_ref[...].astype(F32), gain_ref[...], normed, factor)
        low_ref[...] = total.astype(BF16)
        if keep:
            wide_ref[0][...] = total

    spec = pl.BlockSpec((block, features), lambda j: (j, 0))
    kinds = (BF16, F32) if keep else (BF16,)
    return kernel_call(
        body,
        "norm_backward",
        20 * rows * features,
        (base, gain, x, grad),
        [jax.ShapeDtypeStruct((rows, features), kind) for kind in kinds],
        grid=(rows // block,),
        in_specs=[spec, whole((1, features)), spec, spec],
        out_specs=[spec] * len(kinds),
    )


def feed_forward(h_blocks, c_blocks, w, owners):
    count = len(h_blocks)
    rows, features = h_blocks[0].shape
    units = w.shape[1] // 3
    tile = tile_of(units, 256)
    steps = units // tile

    def body(owners_ref, *refs):
        h_refs, c_refs = refs[:count], refs[count : 2 * count]
        gate_ref, up_ref, down_ref, h_all, c_all, out_ref = refs[2 * count :]

        @pl.when(pl.program_id(0) == 0)
        def _():
            for r in range(count):
                at = pl.multiple_of(owners_ref[r] * rows, rows)
                h_all[pl.ds(at, rows), :] = h_refs[r][...]
                c_all[pl.ds(at, rows), :] = c_refs[r][...]

        gate = mm(h_all[...], gate_ref[...])
        up = mm(h_all[...], up_ref[...])
        grad_hidden = mm(c_all[...], down_ref[...])
        sig = 1.0 / (1.0 + jnp.exp(-gate))
        silu = gate * sig
        out_ref[0] = (grad_hidden * up * (sig * (1.0 + gate * (1.0 - sig)))).astype(BF16)
        out_ref[1] = (grad_hidden * silu).astype(BF16)
        out_ref[2] = (silu * up).astype(BF16)

    total = rows * count
    wide = jax.ShapeDtypeStruct((total, features), BF16)
    return kernel_call(
        body,
        "feed_forward",
        6 * total * features * units,
        (owners, *h_blocks, *c_blocks, w, w, w),
        (wide, wide, jax.ShapeDtypeStruct((3, total, units), BF16)),
        grid_spec=pltpu.PrefetchScalarGridSpec(
            num_scalar_prefetch=1,
            grid=(steps,),
            in_specs=[whole((rows, features))] * (2 * count)
            + [pl.BlockSpec((features, tile), lambda j, _, k=k: (0, k * steps + j)) for k in range(3)],
            out_specs=[whole((total, features))] * 2 + [pl.BlockSpec((3, total, tile), lambda j, _: (0, 0, j))],
        ),
    )


def rows_product(a, leads, w, first, name, owners=None):
    rows, units = a.shape[1:]
    features = w.shape[0]
    tile = tile_of(features, 512 if units * len(leads) > 1024 else 1024)
    count = 1 if owners is None else owners.shape[0]
    block = rows // count
    width = units * len(leads)
    aligned = first % width == 0

    def body(owners_ref, *refs):
        a_refs, w_ref, outs, turned = refs[: len(leads)], refs[len(leads)], refs[len(leads) + 1 : -1], refs[-1]
        if owners is not None:

            @pl.when(pl.program_id(0) == 0)
            def _():
                for r in range(count):
                    at = pl.multiple_of(owners_ref[r] * block, block)
                    for k in range(len(leads)):
                        turned[k, r * block : (r + 1) * block, :] = a_refs[k][0, pl.ds(at, block), :]

        at = 0 if aligned else first
        acc = None
        for k, a_ref in enumerate(a_refs):
            term = outer(a_ref[0] if owners is None else turned[k], w_ref[:, at : at + units])
            acc = term if acc is None else acc + term
            at += units
        for r in range(count):
            outs[r][...] = acc[r * block : (r + 1) * block, :].astype(BF16)

    spec = pl.BlockSpec((tile, width), lambda j, _: (j, first // width))
    if not aligned:
        spec = pl.BlockSpec((tile, w.shape[1]), lambda j, _: (j, 0))
    outs = kernel_call(
        body,
        name,
        2 * rows * features * width,
        [jnp.zeros((1,), jnp.int32) if owners is None else owners] + [a] * len(leads) + [w],
        [jax.ShapeDtypeStruct((block, features), BF16)] * count,
        grid_spec=pltpu.PrefetchScalarGridSpec(
            num_scalar_prefetch=1,
            grid=(features // tile,),
            in_specs=[pl.BlockSpec((1, rows, units), lambda j, _, k=k: (k, 0, 0)) for k in leads] + [spec],
            out_specs=[pl.BlockSpec((block, tile), lambda j, _: (0, j))] * count,
            scratch_shapes=[pltpu.VMEM((len(leads), rows, units) if owners is not None else (1, 16, 128), BF16)],
        ),
    )
    return outs[0] if owners is None else outs


def weight_grad(sides, parts, cube, most, name):
    terms = len(sides[0])
    rows, width = sides[0][0].shape[0], sides[0][0].shape[1] // cube.size
    count = cube.size // 2
    sizes = [n[0][0].shape[-1] for _, n in parts]
    tile = functools.reduce(math.gcd, sizes, most)
    starts = [0]
    for size in sizes:
        starts.append(starts[-1] + size // tile)
    n_sides, n_parts, steps = len(sides), len(parts), starts[-1]
    half_steps = (steps + 1) // 2
    bounds = [0, half_steps, steps]
    place_a, place_b = ([0], [0])
    for m in reversed(cube.hops(0)):
        place_a = place_a + [k | m for k in place_a]
    for m in reversed(cube.hops(1)):
        place_b = place_b + [k | m for k in place_b]
    order_b = [place_a.index(k) for k in place_b]
    cut = count // 2

    def body(places_ref, *refs):
        d_refs = refs[: n_sides * terms * count]
        n_refs = refs[n_sides * terms * count :][: n_parts * terms]
        outs, turned = refs[-5:-1], refs[-1]
        j = pl.program_id(0)

        @pl.when(j == 0)
        def _():
            for k in range(n_sides * terms):
                for q in range(count):
                    turned[k, q * width : (q + 1) * width, :] = d_refs[k * count + q][...].T

        for p, (side, _) in enumerate(parts):
            for half in range(2):
                first, last = max(starts[p], bounds[half]), min(starts[p + 1], bounds[half + 1])
                if first >= last:
                    continue

                @pl.when((j >= first) & (j < last))
                def _(p=p, side=side, half=half):
                    acc = None
                    for t in range(terms):
                        term = mm(turned[side * terms + t], n_refs[p * terms + t][0])
                        acc = term if acc is None else acc + term
                    acc = acc.astype(BF16)
                    for to in range(count):
                        q = order_b[to] if half else to
                        out = outs[2 * half + to // cut]
                        at = to % cut
                        out[at * width : (at + 1) * width, :] = acc[q * width : (q + 1) * width, :]

    def n_spec(p, lead):
        last = starts[p + 1] - starts[p] - 1
        return pl.BlockSpec((1, rows, tile), lambda j, _: (lead, 0, jnp.clip(j - starts[p], 0, last)))

    in_specs = [
        pl.BlockSpec((rows, width), lambda j, p, q=q: (0, p[q])) for _ in range(n_sides * terms) for q in range(count)
    ]
    in_specs += [n_spec(p, lead) for p, (_, n) in enumerate(parts) for _, lead in n]
    operands = [cube.places(0)] + [d for side in sides for d in side for _ in range(count)]
    operands += [a for _, n in parts for a, _ in n]
    out_a = jax.ShapeDtypeStruct((cut * width, half_steps * tile), BF16)
    out_b = jax.ShapeDtypeStruct((cut * width, (steps - half_steps) * tile), BF16)
    spec_a = pl.BlockSpec((cut * width, tile), lambda j, _: (0, jnp.minimum(j, half_steps - 1)))
    spec_b = pl.BlockSpec((cut * width, tile), lambda j, _: (0, jnp.maximum(j - half_steps, 0)))
    keep_a, send_a, keep_b, send_b = kernel_call(
        body,
        name,
        2 * terms * rows * count * width * steps * tile,
        operands,
        [out_a, out_a, out_b, out_b],
        grid_spec=pltpu.PrefetchScalarGridSpec(
            num_scalar_prefetch=1,
            grid=(steps,),
            in_specs=in_specs,
            out_specs=[spec_a, spec_a, spec_b, spec_b],
            scratch_shapes=[pltpu.VMEM((n_sides * terms, count * width, rows), BF16)],
        ),
    )
    return (keep_a, send_a), (keep_b, send_b)


def feed_forward_finals(halves, w_gate, w_up):
    rows, units = w_gate.shape
    widths = [terms[0].shape[1] for terms in halves]
    tile = functools.reduce(math.gcd, widths, units)
    steps, first = units // tile, widths[0] // tile
    flat = [t for terms in halves for t in terms]
    count = len(halves[0])

    def body(*refs):
        terms, (gate_w, up_w, gate_ref, up_ref, down_ref, gain_ref) = refs[: len(flat)], refs[len(flat) :]
        j = pl.program_id(0)

        @pl.when(j == 0)
        def _():
            gain_ref[...] = jnp.zeros_like(gain_ref)

        for k in range(3 * steps):

            @pl.when(j == k)
            def _(k=k):
                total = total32([t[...] for t in (terms[:count] if k < first else terms[count:])])
                if k >= 2 * steps:
                    down_ref[...] = total.T
                else:
                    w_ref, out_ref = (gate_w, gate_ref) if k < steps else (up_w, up_ref)
                    out_ref[...] = total
                    gain_ref[...] += jnp.sum(total * w_ref[...].astype(F32), axis=1, keepdims=True)

    def columns(lo, n):
        return pl.BlockSpec((rows, tile), lambda j: (0, jnp.clip(j - lo, 0, n - 1)))

    wide = jax.ShapeDtypeStruct((rows, units), F32)
    gate_grad, up_grad, down_grad, gain = kernel_call(
        body,
        "feed_forward_finals",
        4 * rows * units * 3,
        (*flat, w_gate, w_up),
        (wide, wide, jax.ShapeDtypeStruct((units, rows), F32), jax.ShapeDtypeStruct((rows, 128), F32)),
        grid=(3 * steps,),
        in_specs=[columns(0, first)] * count
        + [columns(first, widths[1] // tile)] * count
        + [columns(0, steps), columns(steps, steps)],
        out_specs=[
            columns(0, steps),
            columns(steps, steps),
            pl.BlockSpec((tile, rows), lambda j: (jnp.clip(j - 2 * steps, 0, steps - 1), 0)),
            whole((rows, 128)),
        ],
    )
    return gain[:, 0], gate_grad, up_grad, down_grad


def head_columns(heads, kv):
    keys, values = heads * HEAD_DIM, (heads + kv) * HEAD_DIM
    for h in range(heads):
        c = h // (heads // kv)
        yield (
            slice(h * HEAD_DIM, (h + 1) * HEAD_DIM),
            slice(keys + c * HEAD_DIM, keys + (c + 1) * HEAD_DIM),
            slice(values + c * HEAD_DIM, values + (c + 1) * HEAD_DIM),
        )


def segments(ends_ref, count, place):
    found = jnp.zeros_like(place)
    for i in range(count):
        found += (ends_ref[i] <= place).astype(jnp.int32)
    return found


def allowed_pairs(ends_ref, count, j, block, rows):
    query = j * block + lax.broadcasted_iota(jnp.int32, (block, 128), 0)
    key = lax.broadcasted_iota(jnp.int32, (8, rows), 1)
    query_segment, key_segment = segments(ends_ref, count, query)[:, :1], segments(ends_ref, count, key)[:1]
    return (query_segment == key_segment) & (key[:1] <= query[:, :1])


def turn_heads(read, write, columns, cosine, sine):
    step = 2 * HEAD_DIM
    for at in range(0, columns, step):
        cut = slice(at, min(at + step, columns))
        write(cut, turned(read(cut), cosine, sine).astype(BF16))


def attention_forward(ends, owners, x_blocks, gain, w, skip, table, heads, kv):
    blocks = len(x_blocks)
    own_rows, features = x_blocks[0].shape
    rows, width = own_rows * blocks, w.shape[1] - skip
    tile = math.gcd(math.gcd(width, skip), 256)
    steps = width // tile
    block = tile_of(rows, 256)
    turn_width = (heads + kv) * HEAD_DIM
    at_sine = table.shape[1] // 2
    scale = 1.0 / math.sqrt(HEAD_DIM)

    def body(ends_ref, owners_ref, *refs):
        x_refs, (gain_ref, w_ref, table_ref, h_ref, low_ref, out_ref, mass_ref, qkv) = refs[:blocks], refs[blocks:]
        step = pl.program_id(0)

        @pl.when(step == 0)
        def _():
            for r in range(blocks):
                normed, _ = norm_parts(x_refs[r][...].astype(F32))
                at = pl.multiple_of(owners_ref[r] * own_rows, own_rows)
                h_ref[pl.ds(at, own_rows), :] = (normed * gain_ref[...]).astype(BF16)

        for k in range(steps):

            @pl.when(step == k)
            def _(k=k):
                qkv[:, k * tile : (k + 1) * tile] = mm(h_ref[...], w_ref[...])

        @pl.when(step == steps)
        def _():
            def write(cut, v):
                low_ref[:, cut] = v

            turn_heads(lambda cut: qkv[:, cut], write, turn_width, table_ref[:, :at_sine], table_ref[:, at_sine:])
            low_ref[:, turn_width:] = qkv[:, turn_width:].astype(BF16)

        @pl.when(step >= steps)
        def _():
            j = step - steps
            allowed = allowed_pairs(ends_ref, ends.shape[0], j, block, rows)
            here = pl.ds(pl.multiple_of(j * block, block), block)
            lane = lax.broadcasted_iota(jnp.int32, (block, 128), 1)
            mass = jnp.zeros((block, 128), F32)
            for h, (q_at, k_at, v_at) in enumerate(head_columns(heads, kv)):
                scores = outer(low_ref[here, q_at], low_ref[:, k_at]) * scale
                scores = jnp.where(allowed, scores, -1e30)
                row_max = jnp.max(scores, axis=1, keepdims=True)
                weights = jnp.exp(scores - row_max)
                row_sum = jnp.sum(weights, axis=1, keepdims=True)
                weights_low = (weights / row_sum).astype(BF16)
                out_ref[:, q_at] = mm(weights_low, low_ref[:, v_at]).astype(BF16)
                mass = jnp.where(lane == h, row_max + jnp.log(row_sum), mass)
            mass_ref[...] = mass

    return kernel_call(
        body,
        "attention_forward",
        4 * rows * rows * heads * HEAD_DIM + 2 * rows * features * width,
        (ends, owners, *x_blocks, gain, w, table),
        (
            jax.ShapeDtypeStruct((rows, features), BF16),
            jax.ShapeDtypeStruct((rows, width), BF16),
            jax.ShapeDtypeStruct((rows, heads * HEAD_DIM), BF16),
            jax.ShapeDtypeStruct((rows, 128), F32),
        ),
        grid_spec=pltpu.PrefetchScalarGridSpec(
            num_scalar_prefetch=2,
            grid=(steps + rows // block,),
            in_specs=[whole((own_rows, features))] * blocks
            + [
                whole((1, features)),
                pl.BlockSpec((features, tile), lambda j, *_: (0, skip // tile + jnp.minimum(j, steps - 1))),
                whole(table.shape),
            ],
            out_specs=[
                whole((rows, features)),
                whole((rows, width)),
                pl.BlockSpec((block, heads * HEAD_DIM), lambda j, *_: (jnp.maximum(j - steps, 0), 0)),
                pl.BlockSpec((block, 128), lambda j, *_: (jnp.maximum(j - steps, 0), 0)),
            ],
            scratch_shapes=[pltpu.VMEM((rows, width), F32)],
        ),
    )


def attention_backward(ends, grad_rows, w, low, mass, table, heads, kv):
    rows, features = grad_rows.shape
    width, out_width = low.shape[1], heads * HEAD_DIM
    block = tile_of(rows, 256)
    scale = 1.0 / math.sqrt(HEAD_DIM)

    at_sine = table.shape[1] // 2

    def body(ends_ref, grad_ref, w_ref, low_ref, mass_ref, table_ref, out_ref, low_grad, q_grad, k_grad, v_grad):
        j = pl.program_id(0)

        @pl.when(j == 0)
        def _():
            low_grad[...] = mm(grad_ref[...], w_ref[...]).astype(BF16)
            k_grad[...] = jnp.zeros_like(k_grad)
            v_grad[...] = jnp.zeros_like(v_grad)

        allowed = allowed_pairs(ends_ref, ends.shape[0], j, block, rows)
        here = pl.ds(pl.multiple_of(j * block, block), block)
        for h, (q_at, k_at, v_at) in enumerate(head_columns(heads, kv)):
            query, grad = low_ref[here, q_at], low_grad[here, q_at]
            scores = outer(query, low_ref[:, k_at]) * scale
            probs = jnp.exp(jnp.where(allowed, scores, -1e30) - mass_ref[:, h : h + 1])
            grad_probs = outer(grad, low_ref[:, v_at])
            delta = jnp.sum(probs * grad_probs, axis=1, keepdims=True)
            grad_scores = (probs * (grad_probs - delta)).astype(BF16)
            q_grad[:, q_at] = mm(grad_scores, low_ref[:, k_at]) * scale
            c = h // (heads // kv)
            kv_at = slice(c * HEAD_DIM, (c + 1) * HEAD_DIM)
            k_grad[:, kv_at] += inner(grad_scores, query)
            v_grad[:, kv_at] += inner(probs.astype(BF16), grad)

        def write_q(cut, v):
            out_ref[here, cut] = v

        def write_k(cut, v):
            out_ref[:, out_width + cut.start : out_width + cut.stop] = v

        turn_heads(lambda cut: q_grad[:, cut], write_q, out_width, table_ref[here, :at_sine], -table_ref[here, at_sine:])

        @pl.when(j == pl.num_programs(0) - 1)
        def _():
            turn_heads(lambda cut: k_grad[:, cut] * scale, write_k, kv * HEAD_DIM, table_ref[:, :at_sine], -table_ref[:, at_sine:])
            out_ref[:, out_width + kv * HEAD_DIM :] = v_grad[...].astype(BF16)

    return kernel_call(
        body,
        "attention_backward",
        10 * rows * rows * heads * HEAD_DIM + 2 * rows * features * out_width,
        (ends, grad_rows, w, low, mass, table),
        jax.ShapeDtypeStruct((rows, width), BF16),
        grid_spec=pltpu.PrefetchScalarGridSpec(
            num_scalar_prefetch=1,
            grid=(rows // block,),
            in_specs=[
                whole((rows, features)),
                pl.BlockSpec((features, out_width), lambda j, _: (0, 0)),
                whole((rows, width)),
                pl.BlockSpec((block, 128), lambda j, _: (j, 0)),
                whole(table.shape),
            ],
            out_specs=whole((rows, width)),
            scratch_shapes=[
                pltpu.VMEM((rows, out_width), BF16),
                pltpu.VMEM((block, out_width), F32),
                pltpu.VMEM((rows, kv * HEAD_DIM), F32),
                pltpu.VMEM((rows, kv * HEAD_DIM), F32),
            ],
        ),
    )


def per_device(
    dp_size,
    tensor_size,
    tokens,
    seq_lengths,
    seq_group,
    attn_gain,
    w_query,
    w_key,
    w_value,
    w_out,
    mlp_gain,
    w_gate,
    w_up,
    w_down,
    cotangent,
):
    cube = Cube(dp_size)
    line = Line(tensor_size)
    width_q, width_k = w_query.shape[1], w_key.shape[1]
    own_rows = tokens.shape[0]
    row_count = own_rows * tensor_size

    width_out, units = w_out.shape[0], w_gate.shape[1]

    rows_all = line.gather(tokens)
    gains = cube.gather_columns(jnp.stack([attn_gain, mlp_gain])).astype(F32)
    gain_one, gain_two = gains[:1], gains[1:]
    w_attn = lax.all_gather(jnp.concatenate([w_out.T, w_query, w_key, w_value], axis=1), "dp", axis=0, tiled=True)
    w_mlp = lax.all_gather(jnp.concatenate([w_gate, w_up, w_down.T], axis=1), "dp", axis=0, tiled=True)
    incoming_blocks = line.gather(after(cotangent, *rows_all))

    order = Order()
    heads_here = width_q // HEAD_DIM
    kv_here = width_k // HEAD_DIM
    ends, position = layout(seq_lengths, seq_group, cube.me, row_count)
    table = order(lambda p: rope_tables(p, HEAD_DIM), position)
    attn_input, low_qkv, attended, log_mass = order(
        lambda e, x, g, w, t: attention_forward(e, line.owners, x, g, w, width_out, t, heads_here, kv_here),
        ends,
        rows_all,
        gain_one,
        w_attn,
        table,
    )
    attn_input_other = cube.swap(attn_input, 1)
    tokens_f = tokens.astype(F32)

    out_parts = order(
        lambda a, w: rows_product(a, [0], w, 0, "attention_out", line.owners),
        after(attended, incoming_blocks[1])[None],
        w_attn,
    )
    attended_other = cube.swap(attended, 1)
    residual = order(lambda x, *terms: x + total32(terms), tokens_f, *line.scatter(out_parts))
    normed_two, _ = norm_parts(residual)
    mlp_blocks = line.gather((normed_two * gain_two).astype(BF16))

    mlp_input, incoming, unit_grads = order(
        lambda h, c, w: feed_forward(h, c, w, line.owners),
        mlp_blocks,
        incoming_blocks,
        after(w_mlp, attn_input_other, attended_other),
    )
    mlp_others = [cube.swap(v, 1) for v in (mlp_input, incoming, unit_grads)]
    two_parts = order(lambda a, w: rows_product(a, [0, 1], w, 0, "feed_forward_rows_grad"), unit_grads, w_mlp)
    two_sum = lax.psum_scatter(two_parts, "tensor", scatter_dimension=0, tiled=True)

    def mlp_grad(h, c, n, h_other, c_other, n_other):
        parts = [(side, [(n, lead), (n_other, lead)]) for side, lead in ((0, 0), (0, 1), (1, 2))]
        return weight_grad([[h, h_other], [c, c_other]], parts, cube, 512, "feed_forward_grad")

    mlp_pairs = cube.first_hop(order(mlp_grad, mlp_input, incoming, unit_grads, *mlp_others))
    grad_low, grad_residual = order(
        lambda *a: norm_backward(*a, True), cotangent, gain_two, residual, two_sum
    )
    grad_attn_rows = lax.all_gather(grad_low, "tensor", axis=0, tiled=True)
    block_parts = order(lambda a, w: rows_product(a, [2], w, 2 * units, "block_out"), unit_grads, w_mlp)
    block_parts, grad_attn_rows = lax.optimization_barrier((block_parts, grad_attn_rows))
    block_sum = lax.psum_scatter(block_parts, "tensor", scatter_dimension=0, tiled=True)
    rows_other = cube.swap(grad_attn_rows, 1)

    grad_qkv = order(
        lambda *a: attention_backward(*a, heads_here, kv_here), ends, grad_attn_rows, w_attn, low_qkv, log_mass, table
    )
    mlp_terms = cube.other_hops(mlp_pairs, order)
    one_parts = order(
        lambda a, w: rows_product(a, [0], w, width_out, "attention_rows_grad"), grad_qkv[None], w_attn
    )
    one_sum = lax.psum_scatter(after(one_parts, block_sum), "tensor", scatter_dimension=0, tiled=True)


    def attn_grad(y, y_other, h, h_other, a, a_other, g, g_other):
        parts = [(0, [(a[None], 0), (a_other[None], 0)]), (1, [(g[None], 0), (g_other[None], 0)])]
        return weight_grad([[y, y_other], [h, h_other]], parts, cube, 256, "attention_grad")

    attn_pairs = cube.first_hop(
        order(
            attn_grad,
            grad_attn_rows,
            rows_other,
            attn_input,
            attn_input_other,
            attended,
            attended_other,
            grad_qkv,
            cube.swap(grad_qkv, 1),
        )
    )
    block_out = order(lambda x, t: (x + t.astype(F32)).astype(BF16), residual, block_sum)
    attn_terms = cube.other_hops(attn_pairs, order)

    def gain_terms(*pairs):
        return functools.reduce(lambda a, b: a + b, [jnp.sum(w.astype(F32) * g, axis=1) for w, g in pairs])

    mlp_gain_terms, gate_grad, up_grad, down_grad = order(feed_forward_finals, mlp_terms, w_gate, w_up)
    (grad_tokens,) = order(lambda *a: norm_backward(*a, False), grad_residual, gain_one, tokens, one_sum)
    attn_sum = block_sum32(attn_terms)
    out_grad, qkv_grad = attn_sum[:, :width_out].T, attn_sum[:, width_out:]
    query_grad = qkv_grad[:, :width_q]
    key_grad = qkv_grad[:, width_q : width_q + width_k]
    value_grad = qkv_grad[:, width_q + width_k :]
    attn_gain_terms = gain_terms((w_query, query_grad), (w_key, key_grad), (w_value, value_grad))
    gain_sums = line.total(jnp.stack([attn_gain_terms, mlp_gain_terms]))
    attn_gain_grad = gain_sums[0] / attn_gain.astype(F32)
    mlp_gain_grad = gain_sums[1] / mlp_gain.astype(F32)
    return (
        block_out,
        grad_tokens,
        attn_gain_grad,
        query_grad,
        key_grad,
        value_grad,
        out_grad,
        mlp_gain_grad,
        gate_grad,
        up_grad,
        down_grad,
    )


def solution(mesh):
    return jax.shard_map(
        functools.partial(per_device, mesh.shape["dp"], mesh.shape["tensor"]),
        mesh=mesh,
        in_specs=(
            P(("dp", "tensor"), None),
            P(),
            P(),
            P("dp"),
            P("dp", "tensor"),
            P("dp", "tensor"),
            P("dp", "tensor"),
            P("tensor", "dp"),
            P("dp"),
            P("dp", "tensor"),
            P("dp", "tensor"),
            P("tensor", "dp"),
            P(("dp", "tensor"), None),
        ),
        out_specs=(
            P(("dp", "tensor"), None),
            P(("dp", "tensor"), None),
            P("dp"),
            P("dp", "tensor"),
            P("dp", "tensor"),
            P("dp", "tensor"),
            P("tensor", "dp"),
            P("dp"),
            P("dp", "tensor"),
            P("dp", "tensor"),
            P("tensor", "dp"),
        ),
        check_vma=False,
    )
```
